512 devices in a mesh: tile: 64 (over x, z), hid: 8 (over y, core).
Axes of the slice: x: 4, y: 4, z: 16, core: 2. Of those that a mesh axis runs over, the one named last changes fastest.
Arguments:
- nodes: bfloat16 [16384, 512], P('tile'), may hold values from -6 to 6
- edges: bfloat16 [49152, 512], P('tile'), may hold values from -6 to 6
- node_cotangent: bfloat16 [16384, 512], P('tile'), may hold values from -6 to 6
- edge_first: bfloat16 [1536, 512], P(None, 'hid'), may hold values from -0.15625 to 0.15625
- edge_second: bfloat16 [512, 512], P('hid'), may hold values from -0.25 to 0.25
- node_first: bfloat16 [1024, 512], P(None, 'hid'), may hold values from -0.1875 to 0.1875
- node_second: bfloat16 [512, 512], P('hid'), may hold values from -0.25 to 0.25
- sender: int32 [49152], P('tile'), may hold values from 0 to 767
- receiver_pos: int32 [49152], P('tile'), may hold values from 0 to 127
- block_tile: int32 [384], P('tile'), may hold values from 0 to 1
- live_blocks: int32 [64], P('tile'), may hold values from 3 to 6, as said below
- send_rows: int32 [64, 64, 8], P('tile'), may hold values from 0 to 255
Outputs:
- node_out: bfloat16 [16384, 512], P('tile')
- node_grad: bfloat16 [16384, 512], P('tile')
- edge_first_grad: float32 [1536, 512], P('tile', 'hid')
The draws below stay inside these ranges and needn't reach their ends.
Inputs may be any that keep to these rules, and one draw needn't show every extreme that they name: Blocks 0 to live_blocks[d] - 1 of device d carry its edges, the later blocks none; some device has all 6 blocks live.
All inputs are finite; a program needn't handle non-finite values.
Results may differ from the reference program's by a relative error of at most 0.013.
Values may be sent and summed in bfloat16 or wider, within the bound.
No kernel may reach another device: no remote copies, remote signals or barrier semaphores. Data moves between devices by JAX's collectives and lax.ppermute only.
A program may use at most 64 MiB of HBM per device.

```python
import jax
import jax.numpy as jnp
from jax import lax

D = 512
H = 512
TILE = 128
TILES_DEV = 2
BLK_DEV = 6
CAP = 8
NODE_DEV = 256
EDGE_DEV = 768
HALO = 512
NODES = 16384
EDGES = 49152
BLOCKS = 384
N_TILE = 64


def draw_live_blocks(key, part):
    key = jax.random.fold_in(key, 11)
    key_counts, key_full = jax.random.split(key)
    counts = jax.random.randint(key_counts, (N_TILE,), BLK_DEV // 2, BLK_DEV + 1)
    full_device = jax.random.randint(key_full, (), 0, N_TILE)
    return jnp.where(jnp.arange(N_TILE) == full_device, BLK_DEV, counts).astype(jnp.int32)


def place_ends(drawn, own_key, smallest, largest):
    longest = drawn.shape.index(max(drawn.shape))
    spots = []
    for shift in (0, 1):
        where = [jax.random.randint(jax.random.fold_in(own_key, axis), (), 0, length) for axis, length in enumerate(drawn.shape)]
        where[longest] = (where[longest] + shift) % drawn.shape[longest]
        spots.append(tuple(where))
    return drawn.at[spots[0]].set(smallest).at[spots[1]].set(largest)


def levels(own_key, extent, shards, least, high):
    def one(axis_at, shards_of):
        steps = jax.random.uniform(jax.random.fold_in(jax.random.fold_in(own_key, 6), axis_at), (shards_of,), jnp.float32, least / len(shards), high / len(shards))
        return jnp.repeat(jnp.exp(steps), extent[axis_at] // shards_of).reshape((-1,) + (1,) * (len(extent) - axis_at - 1))

    gain = one(*shards[0])
    for cut in shards[1:]:
        gain = gain * one(*cut)
    return gain


def noise(key, shape, deviation, limit, cuts=(), kind=jnp.bfloat16):
    drawn = deviation * jax.random.normal(key, shape, jnp.float32)
    if cuts:
        drawn = drawn * levels(key, shape, cuts, -0.22, 0.18)
    return jnp.clip(drawn, -limit, limit).astype(kind)


def setup_inputs(seed: int = 0) -> dict:
    seeds = jax.random.split(jax.random.key(seed), 13)
    return {
        "nodes": noise(seeds[0], (NODES, D), 1.0, 6.0, ((0, 64),)),
        "edges": noise(seeds[1], (EDGES, D), 1.0, 6.0, ((0, 64),)),
        "node_cotangent": noise(seeds[2], (NODES, D), 1.0, 6.0, ((0, 64),)),
        "edge_first": noise(seeds[3], (3 * D, H), (3 * D) ** -0.5, 0.15625, ((1, 8),)),
        "edge_second": noise(seeds[4], (H, D), H ** -0.5, 0.25, ((0, 8),)),
        "node_first": noise(seeds[5], (2 * D, H), (2 * D) ** -0.5, 0.1875, ((1, 8),)),
        "node_second": noise(seeds[6], (H, D), H ** -0.5, 0.25, ((0, 8),)),
        "sender": place_ends(jax.random.randint(seeds[7], (EDGES,), 0, NODE_DEV + HALO), jax.random.fold_in(seeds[7], 1), 0, (NODE_DEV + HALO) - 1).astype(jnp.int32),
        "receiver_pos": place_ends(jax.random.randint(seeds[8], (EDGES,), 0, TILE), jax.random.fold_in(seeds[8], 1), 0, TILE - 1).astype(jnp.int32),
        "block_tile": place_ends(jax.random.randint(seeds[9], (BLOCKS,), 0, TILES_DEV), jax.random.fold_in(seeds[9], 1), 0, TILES_DEV - 1).astype(jnp.int32),
        "live_blocks": draw_live_blocks(jax.random.fold_in(seeds[12], 71), 0),
        "send_rows": place_ends(jax.random.randint(seeds[11], (N_TILE, N_TILE, CAP), 0, NODE_DEV), jax.random.fold_in(seeds[11], 1), 0, NODE_DEV - 1).astype(jnp.int32),
    }


epsilon = 1e-05

def layer_norm(values):
    centre = lax.optimization_barrier(jnp.mean(values, axis=-1, keepdims=True))
    shifted = values - centre
    variance = lax.optimization_barrier(jnp.mean(shifted * shifted, axis=-1, keepdims=True))
    return shifted * lax.rsqrt(variance + epsilon)

def silu_slope(preact):
    sigmoid_value = jax.nn.sigmoid(preact)
    return sigmoid_value * (1.0 + preact * (1.0 - sigmoid_value))

def reference(nodes, edges, node_cotangent, edge_first, edge_second, node_first, node_second, sender, receiver_pos, block_tile, live_blocks, send_rows):
    peer_base = (jnp.arange(N_TILE, dtype=jnp.int32) * NODE_DEV)[:, None]

    def device_pass(state, device):
        grad_sum, weight_sum = state
        row_base = (device * NODE_DEV).astype(jnp.int32)
        own_rows = lax.dynamic_slice_in_dim(nodes, row_base, NODE_DEV, 0)
        halo_index = (peer_base + jnp.take(send_rows, device, axis=1)).reshape(-1).astype(jnp.int32)
        node_table = jnp.concatenate([own_rows, jnp.take(nodes, halo_index, axis=0)], axis=0)
        edge_base = (device * EDGE_DEV).astype(jnp.int32)
        edge_d = lax.dynamic_slice_in_dim(edges, edge_base, EDGE_DEV, 0)
        send_d = lax.dynamic_slice_in_dim(sender, edge_base, EDGE_DEV, 0)
        pos_d = lax.dynamic_slice_in_dim(receiver_pos, edge_base, EDGE_DEV, 0)
        tiles_d = lax.dynamic_slice_in_dim(block_tile, (device * BLK_DEV).astype(jnp.int32), BLK_DEV, 0)
        receiver = (jnp.repeat(tiles_d, TILE) * TILE + pos_d).astype(jnp.int32)
        live_rows = jnp.repeat(jnp.arange(BLK_DEV, dtype=jnp.int32) < live_blocks[device], TILE)
        stacked = jnp.concatenate([edge_d, jnp.take(node_table, send_d, axis=0), jnp.take(own_rows, receiver, axis=0)], axis=1)
        preact = jnp.dot(stacked, edge_first, preferred_element_type=jnp.float32)
        hidden = jax.nn.silu(preact).astype(jnp.bfloat16)
        edge_sum = jnp.dot(hidden, edge_second, preferred_element_type=jnp.float32)
        edge_norm, edge_back = jax.vjp(layer_norm, edge_sum)
        edge_new = (edge_d.astype(jnp.float32) + edge_norm).astype(jnp.bfloat16)
        masked_new = jnp.where(live_rows[:, None], edge_new.astype(jnp.float32), jnp.float32(0.0))
        aggregated = jax.ops.segment_sum(masked_new, receiver, num_segments=NODE_DEV)
        node_in = jnp.concatenate([own_rows, aggregated.astype(jnp.bfloat16)], axis=1)
        preact_node = jnp.dot(node_in, node_first, preferred_element_type=jnp.float32)
        hidden_node = jax.nn.silu(preact_node).astype(jnp.bfloat16)
        node_sum = jnp.dot(hidden_node, node_second, preferred_element_type=jnp.float32)
        node_norm, node_back = jax.vjp(layer_norm, node_sum)
        node_new = (own_rows.astype(jnp.float32) + node_norm).astype(jnp.bfloat16)
        cotangent = lax.dynamic_slice_in_dim(node_cotangent, row_base, NODE_DEV, 0).astype(jnp.float32)
        d_node_sum = node_back(cotangent)[0].astype(jnp.bfloat16)
        d_preact_node = (jnp.dot(d_node_sum, node_second.T, preferred_element_type=jnp.float32) * silu_slope(preact_node)).astype(jnp.bfloat16)
        d_node_in = jnp.dot(d_preact_node, node_first.T, preferred_element_type=jnp.float32)
        d_aggregated = d_node_in[:, D:].astype(jnp.bfloat16)
        d_edge_new = jnp.where(live_rows[:, None], jnp.take(d_aggregated, receiver, axis=0).astype(jnp.float32), jnp.float32(0.0))
        d_edge_sum = edge_back(d_edge_new)[0].astype(jnp.bfloat16)
        d_preact = (jnp.dot(d_edge_sum, edge_second.T, preferred_element_type=jnp.float32) * silu_slope(preact)).astype(jnp.bfloat16)
        weight_part = jnp.dot(stacked.T, d_preact, preferred_element_type=jnp.float32)
        d_stacked = jnp.dot(d_preact, edge_first[D:].T, preferred_element_type=jnp.float32)
        table_grad = jax.ops.segment_sum(d_stacked[:, :D], send_d, num_segments=NODE_DEV + HALO)
        own_grad = cotangent + d_node_in[:, :D] + jax.ops.segment_sum(d_stacked[:, D:], receiver, num_segments=NODE_DEV) + table_grad[:NODE_DEV]
        current = lax.dynamic_slice_in_dim(grad_sum, row_base, NODE_DEV, 0)
        grad_sum = lax.dynamic_update_slice_in_dim(grad_sum, current + own_grad, row_base, 0)
        grad_sum = grad_sum.at[halo_index].add(table_grad[NODE_DEV:])
        return ((grad_sum, weight_sum + weight_part), node_new)
    initial = (jnp.zeros((NODES, D), jnp.float32), jnp.zeros((3 * D, H), jnp.float32))
    (grad_sum, weight_sum), node_blocks = lax.scan(device_pass, initial, jnp.arange(N_TILE, dtype=jnp.int32))
    return (node_blocks.reshape(NODES, D), grad_sum.astype(jnp.bfloat16), weight_sum)
```

```python
import jax
import jax.numpy as jnp
from jax import lax
from jax.experimental import pallas as pl
from jax.experimental.pallas import tpu as pltpu
from jax.sharding import Mesh, PartitionSpec as P

TILE = 128
epsilon = 1e-05
bf16 = jnp.bfloat16
f32 = jnp.float32
VMEM_LIMIT = 56 * 1024 * 1024
CHUNK = 32


def nn(a, b):
    return lax.dot_general(a, b, (((1,), (0,)), ((), ())), preferred_element_type=f32)


def nt(a, b):
    return lax.dot_general(a, b, (((1,), (1,)), ((), ())), preferred_element_type=f32)


def tn(a, b):
    return lax.dot_general(a, b, (((0,), (0,)), ((), ())), preferred_element_type=f32)


def onehot_rows(index_row, count):
    n = index_row.shape[1]
    column = jnp.broadcast_to(index_row, (TILE, n)).T
    lanes = lax.broadcasted_iota(jnp.int32, (n, TILE), 1)
    return jnp.concatenate(
        [(column == lanes + k * TILE).astype(f32).astype(bf16) for k in range(count // TILE)],
        axis=1,
    )


def onehot_columns(index_row, count):
    n = index_row.shape[1]
    rows = lax.broadcasted_iota(jnp.int32, (count, n), 0)
    return (index_row == rows).astype(f32).astype(bf16)


def supply_kernel(nodes, send, first, second, node_first, node_second, supply, weights):
    core = lax.axis_index("core")
    half = nodes.shape[1] // 2
    hot = onehot_rows(send[...], nodes.shape[0])
    columns = pl.ds(pl.multiple_of(core * half, half), half)
    supply[...] = nn(hot, nodes[:, columns]).astype(bf16)
    weights[...] = jnp.concatenate(
        [
            first[...].astype(f32).T.astype(bf16),
            node_first[...].astype(f32).T.astype(bf16),
            second[...],
            node_second[...],
        ],
        axis=1,
    )


def sigmoid(v):
    return 0.5 * jnp.tanh(0.5 * v) + 0.5


def normed(v):
    centre = jnp.mean(v, axis=-1, keepdims=True)
    shifted = v - centre
    variance = jnp.mean(shifted * shifted, axis=-1, keepdims=True)
    scale = lax.rsqrt(variance + epsilon)
    return shifted * scale, scale


def normed_back(g, unit, scale):
    return scale * (
        g
        - jnp.mean(g, axis=-1, keepdims=True)
        - unit * jnp.mean(g * unit, axis=-1, keepdims=True)
    )


def by_rows(total, body):
    def step(i, carry):
        body(pl.ds(pl.multiple_of(i * CHUNK, CHUNK), CHUNK))
        return carry

    lax.fori_loop(0, total // CHUNK, step, 0, unroll=2)


def step_kernel(
    tiles,
    live,
    nodes,
    edges,
    cotangent,
    halo,
    weights,
    sender,
    position,
    node_out,
    outgoing,
    base,
    table,
    stacked,
    wide,
    slope,
    unit,
    scale,
    low,
    received,
):
    d = nodes.shape[1]
    half = d // 2
    n = nodes.shape[0]
    e = edges.shape[0]
    h = halo.shape[0] // 2
    core = lax.axis_index("core")
    share = 2 * lax.axis_index("y") + core
    first = weights.at[:, : 3 * d]
    node_first = weights.at[:, 3 * d : 5 * d]
    second = weights.at[:, 5 * d : 6 * d]
    node_second = weights.at[:, 6 * d : 7 * d]

    table[:n] = nodes[...]
    table[n:, :half] = halo[:h]
    table[n:, half:] = halo[h:]
    receiver = jnp.concatenate(
        [
            jnp.where(
                b < live[0], position[:, b * TILE : (b + 1) * TILE] + tiles[b] * TILE, -1
            )
            for b in range(e // TILE)
        ],
        axis=1,
    )
    received[...] = onehot_rows(receiver, n)
    stacked[:, :d] = edges[...]
    stacked[:, d : 2 * d] = nn(onehot_rows(sender[...], n + h), table[...]).astype(bf16)
    stacked[:, 2 * d :] = nn(received[...], nodes[...]).astype(bf16)

    wide[...] = nt(stacked[...], first[...])

    def activate(rows):
        v = wide[rows, :]
        s = sigmoid(v)
        low[rows, :] = (v * s).astype(bf16)
        slope[rows, :] = s * (1.0 + v * (1.0 - s))

    by_rows(e, activate)
    wide[...] = nn(low[...], second[...])

    def normalise(rows):
        u, r = normed(wide[rows, :])
        unit[rows, :] = u
        scale[rows, :] = jnp.broadcast_to(r, (CHUNK, TILE))
        low[rows, :] = (edges[rows, :].astype(f32) + u).astype(bf16)

    by_rows(e, normalise)
    back = onehot_columns(receiver, n)
    aggregated = nn(back, low[...]).astype(bf16)

    preact_node = nt(jnp.concatenate([nodes[...], aggregated], axis=1), node_first[...])
    s = sigmoid(preact_node)
    hidden_node = (preact_node * s).astype(bf16)
    node_unit, node_scale = normed(nn(hidden_node, node_second[...]))
    node_out[...] = (nodes[...].astype(f32) + node_unit).astype(bf16)
    d_node_sum = normed_back(cotangent[...].astype(f32), node_unit, node_scale).astype(bf16)
    d_preact_node = (
        nt(d_node_sum, node_second[...]) * (s * (1.0 + preact_node * (1.0 - s)))
    ).astype(bf16)
    d_aggregated = nn(d_preact_node, node_first[:, d:]).astype(bf16)
    columns = pl.ds(pl.multiple_of(core * half, half), half)
    base[...] = cotangent[:, columns].astype(f32) + nn(
        d_preact_node, weights[:, pl.ds(pl.multiple_of(3 * d + core * half, half), half)]
    )

    wide[...] = nn(received[...], d_aggregated)

    def denormalise(rows):
        low[rows, :] = normed_back(wide[rows, :], unit[rows, :], scale[rows, :1]).astype(bf16)

    by_rows(e, denormalise)
    wide[...] = nt(low[...], second[...])

    def deactivate(rows):
        low[rows, :] = (wide[rows, :] * slope[rows, :]).astype(bf16)

    by_rows(e, deactivate)

    units = weights.shape[0]
    own = units // 8
    pick = (
        lax.broadcasted_iota(jnp.int32, (units, own), 0)
        == lax.broadcasted_iota(jnp.int32, (units, own), 1) + share * own
    )
    d_own = nn(low[...], pick.astype(f32).astype(bf16))
    grad = tn(d_own.astype(bf16), stacked[...]).T.reshape(64, 3 * d // 64, own)
    left = grad[:, :16]
    right = jnp.concatenate([grad[:, 16:], jnp.zeros((64, 8, own), f32)], axis=1)
    packed = jnp.concatenate([left, right], axis=2)

    d_sender = nn(
        low[...], weights[:, pl.ds(pl.multiple_of(d + core * half, half), half)]
    ).astype(bf16)
    d_receiver = nn(
        low[...], weights[:, pl.ds(pl.multiple_of(2 * d + core * half, half), half)]
    ).astype(bf16)
    table_grad = nn(onehot_columns(sender[...], n + h), d_sender)
    base[...] += table_grad[:n] + nn(back, d_receiver)
    outgoing[...] = jnp.concatenate(
        [
            table_grad[n:, :TILE].reshape(64, 8, TILE),
            table_grad[n:, TILE:].reshape(64, 8, TILE),
            packed,
        ],
        axis=1,
    ).astype(bf16)


def finish_kernel(incoming, base, send, node_grad, first_grad):
    values = incoming[...].astype(f32)
    rows = values.shape[0] * 8
    returned = jnp.concatenate(
        [values[:, :8].reshape(rows, TILE), values[:, 8:16].reshape(rows, TILE)], axis=1
    ).astype(bf16)
    hot = onehot_columns(send[...], base.shape[0])
    node_grad[...] = (base[...] + nn(hot, returned)).astype(bf16)
    total = jnp.sum(values[:, 16:], axis=0)
    own = first_grad.shape[1]
    first_grad[...] = jnp.concatenate([total[:, :own], total[:8, own:]], axis=0)


def per_device(
    nodes,
    edges,
    node_cotangent,
    edge_first,
    edge_second,
    node_first,
    node_second,
    sender,
    receiver_pos,
    block_tile,
    live_blocks,
    send_rows,
):
    n, d = nodes.shape
    e = edges.shape[0]
    half = d // 2
    peers, slots = send_rows.shape[1], send_rows.shape[2]
    h = peers * slots
    shares = lax.axis_size(("y", "core"))
    units = edge_second.shape[0] * shares
    own = edge_second.shape[0]
    width = edge_first.shape[0] + node_first.shape[0] + 2 * d
    vmem = pl.BlockSpec(memory_space=pltpu.VMEM)
    smem = pl.BlockSpec(memory_space=pltpu.SMEM)
    params = pltpu.CompilerParams(vmem_limit_bytes=VMEM_LIMIT)
    send = send_rows.reshape(1, h)

    supply, share = pl.pallas_call(
        supply_kernel,
        out_shape=(
            jax.ShapeDtypeStruct((h, half), bf16),
            jax.ShapeDtypeStruct((own, width), bf16),
        ),
        in_specs=[vmem] * 6,
        out_specs=(vmem, vmem),
        compiler_params=params,
        name="supply",
    )(nodes, send, edge_first, edge_second, node_first, node_second)
    weights = lax.all_gather(share, ("y", "core"), axis=0, tiled=True)
    received = lax.all_to_all(
        supply.reshape(peers, slots, half), ("x", "z"), split_axis=0, concat_axis=0, tiled=True
    ).reshape(h, half)
    halo = lax.all_gather(received, "core", axis=0, tiled=True)

    node_out, outgoing, base = pl.pallas_call(
        step_kernel,
        out_shape=(
            jax.ShapeDtypeStruct((n, d), bf16),
            jax.ShapeDtypeStruct((peers, 32, TILE), bf16),
            jax.ShapeDtypeStruct((n, half), f32),
        ),
        in_specs=[smem, smem] + [vmem] * 7,
        out_specs=(vmem, vmem, vmem),
        scratch_shapes=[
            pltpu.VMEM((n + h, d), bf16),
            pltpu.VMEM((e, 3 * d), bf16),
            pltpu.VMEM((e, units), f32),
            pltpu.VMEM((e, units), f32),
            pltpu.VMEM((e, d), f32),
            pltpu.VMEM((e, TILE), f32),
            pltpu.VMEM((e, units), bf16),
            pltpu.VMEM((e, n), bf16),
        ],
        compiler_params=params,
        name="step",
    )(
        block_tile,
        live_blocks,
        nodes,
        edges,
        node_cotangent,
        halo,
        weights,
        sender.reshape(1, e),
        receiver_pos.reshape(1, e),
    )
    incoming = lax.all_to_all(outgoing, ("x", "z"), split_axis=0, concat_axis=0, tiled=True)
    half_grad, first_grad = pl.pallas_call(
        finish_kernel,
        out_shape=(
            jax.ShapeDtypeStruct((n, half), bf16),
            jax.ShapeDtypeStruct((edge_first.shape[0] // peers, own), f32),
        ),
        in_specs=[vmem] * 3,
        out_specs=(vmem, vmem),
        compiler_params=params,
        name="finish",
    )(incoming, base, send)
    node_grad = lax.all_gather(half_grad, "core", axis=1, tiled=True)
    return (node_out, node_grad, first_grad)


def solution(mesh):
    devices = mesh.devices
    tiles, shares = devices.shape
    fine = Mesh(devices.reshape(4, tiles // 4, shares // 2, 2), ("x", "z", "y", "core"))
    tile = ("x", "z")
    hid = ("y", "core")
    in_specs = (
        P(tile, None),
        P(tile, None),
        P(tile, None),
        P(None, hid),
        P(hid, None),
        P(None, hid),
        P(hid, None),
        P(tile),
        P(tile),
        P(tile),
        P(tile),
        P(tile, None, None),
    )
    out_specs = (P(tile, None), P(tile, None), P(tile, hid))
    return jax.shard_map(
        per_device, mesh=fine, in_specs=in_specs, out_specs=out_specs, check_vma=False
    )
```

```python
import jax
import jax.numpy as jnp
from jax import lax
from jax.experimental import pallas as pl
from jax.experimental.pallas import tpu as pltpu
from jax.sharding import Mesh, PartitionSpec as P

TILE = 128
epsilon = 1e-05
bf16 = jnp.bfloat16
f32 = jnp.float32
VMEM_LIMIT = 56 * 1024 * 1024
CHUNK = 32


def nn(a, b):
    return lax.dot_general(a, b, (((1,), (0,)), ((), ())), preferred_element_type=f32)


def nt(a, b):
    return lax.dot_general(a, b, (((1,), (1,)), ((), ())), preferred_element_type=f32)


def tn(a, b):
    return lax.dot_general(a, b, (((0,), (0,)), ((), ())), preferred_element_type=f32)


def onehot_rows(index_row, count):
    n = index_row.shape[1]
    column = jnp.broadcast_to(index_row, (TILE, n)).T
    lanes = lax.broadcasted_iota(jnp.int32, (n, TILE), 1)
    return jnp.concatenate(
        [(column == lanes + k * TILE).astype(f32).astype(bf16) for k in range(count // TILE)],
        axis=1,
    )


def onehot_columns(index_row, count):
    n = index_row.shape[1]
    rows = lax.broadcasted_iota(jnp.int32, (count, n), 0)
    return (index_row == rows).astype(f32).astype(bf16)


def flat_row(rows):
    return jnp.concatenate([rows[i : i + 1] for i in range(rows.shape[0])], axis=1)


def slot_order(slots, peers):
    count = slots * peers
    row = lax.broadcasted_iota(jnp.int32, (count, count), 0)
    column = lax.broadcasted_iota(jnp.int32, (count, count), 1)
    return ((row % slots) * peers + row // slots == column).astype(f32).astype(bf16)


def supply_kernel(nodes, send, first, second, node_first, node_second, supply, weights):
    core = lax.axis_index("core")
    half = nodes.shape[1] // 2
    hot = onehot_rows(flat_row(send[...]), nodes.shape[0])
    columns = pl.ds(pl.multiple_of(core * half, half), half)
    rows = nn(hot, nodes[:, columns]).astype(bf16)
    supply[...] = nn(slot_order(*send.shape), rows).astype(bf16)
    at = 0
    for part in (first, node_first, second, node_second):
        weights[:, at : at + part.shape[1]] = part[...]
        at += part.shape[1]


def sigmoid(v):
    return 0.5 * jnp.tanh(0.5 * v) + 0.5


def normed(v):
    centre = jnp.mean(v, axis=-1, keepdims=True)
    shifted = v - centre
    variance = jnp.mean(shifted * shifted, axis=-1, keepdims=True)
    scale = lax.rsqrt(variance + epsilon)
    return shifted * scale, scale


def normed_back(g, unit, scale):
    return scale * (
        g
        - jnp.mean(g, axis=-1, keepdims=True)
        - unit * jnp.mean(g * unit, axis=-1, keepdims=True)
    )


def by_rows(total, body):
    def step(i, carry):
        body(pl.ds(pl.multiple_of(i * CHUNK, CHUNK), CHUNK))
        return carry

    lax.fori_loop(0, total // CHUNK, step, 0, unroll=2)


def step_kernel(
    tiles,
    live,
    nodes,
    edges,
    cotangent,
    halo,
    pair,
    near,
    far,
    near_other,
    far_other,
    sender,
    position,
    node_out,
    outgoing,
    base,
    table,
    stacked,
    wide,
    slope,
    unit,
    scale,
    low,
    received,
    weights,
):
    d = nodes.shape[1]
    half = d // 2
    n = nodes.shape[0]
    e = edges.shape[0]
    h = halo.shape[0] // 2
    core = lax.axis_index("core")
    first = pl.ds(0, 3 * d)
    node_first = pl.ds(3 * d, 2 * d)
    second = pl.ds(5 * d, d)
    node_second = pl.ds(6 * d, d)
    parts = (pair, near, far, near_other, far_other)
    units = 0
    for piece in parts:
        weights[units : units + piece.shape[0], :] = piece[...]
        units += piece.shape[0]

    def to_units(x, columns):
        return nt(x, weights[:, columns])

    def from_units(x, columns):
        return nn(x, weights[:, columns])

    table[:n] = nodes[...]
    table[n:, :half] = halo[:h]
    table[n:, half:] = halo[h:]
    receiver = jnp.concatenate(
        [
            jnp.where(
                b < live[0], position[b : b + 1, :] + tiles[b] * TILE, -1
            )
            for b in range(e // TILE)
        ],
        axis=1,
    )
    received[...] = onehot_rows(receiver, n)
    senders = flat_row(sender[...])
    stacked[:, :d] = edges[...]
    stacked[:, d : 2 * d] = nn(onehot_rows(senders, n + h), table[...]).astype(bf16)
    stacked[:, 2 * d :] = nn(received[...], nodes[...]).astype(bf16)

    wide[...] = to_units(stacked[...], first)

    def activate(rows):
        v = wide[rows, :]
        s = sigmoid(v)
        low[rows, :] = (v * s).astype(bf16)
        slope[rows, :] = s * (1.0 + v * (1.0 - s))

    by_rows(e, activate)
    wide[...] = from_units(low[...], second)

    def normalise(rows):
        u, r = normed(wide[rows, :])
        unit[rows, :] = u
        scale[rows, :] = jnp.broadcast_to(r, (CHUNK, TILE))
        low[rows, :] = (edges[rows, :].astype(f32) + u).astype(bf16)

    by_rows(e, normalise)
    back = onehot_columns(receiver, n)
    aggregated = nn(back, low[...]).astype(bf16)

    preact_node = to_units(jnp.concatenate([nodes[...], aggregated], axis=1), node_first)
    s = sigmoid(preact_node)
    hidden_node = (preact_node * s).astype(bf16)
    node_unit, node_scale = normed(from_units(hidden_node, node_second))
    node_out[...] = (nodes[...].astype(f32) + node_unit).astype(bf16)
    d_node_sum = normed_back(cotangent[...].astype(f32), node_unit, node_scale).astype(bf16)
    d_preact_node = (
        to_units(d_node_sum, node_second) * (s * (1.0 + preact_node * (1.0 - s)))
    ).astype(bf16)
    d_aggregated = from_units(d_preact_node, pl.ds(4 * d, d)).astype(bf16)
    columns = pl.ds(pl.multiple_of(core * half, half), half)
    base[...] = cotangent[:, columns].astype(f32) + from_units(
        d_preact_node, pl.ds(pl.multiple_of(3 * d + core * half, half), half)
    )

    wide[...] = nn(received[...], d_aggregated)

    def denormalise(rows):
        low[rows, :] = normed_back(wide[rows, :], unit[rows, :], scale[rows, :1]).astype(bf16)

    by_rows(e, denormalise)
    wide[...] = to_units(low[...], second)

    def deactivate(rows):
        low[rows, :] = (wide[rows, :] * slope[rows, :]).astype(bf16)

    by_rows(e, deactivate)

    own = units // 8
    pick = (
        lax.broadcasted_iota(jnp.int32, (units, own), 0)
        == lax.broadcasted_iota(jnp.int32, (units, own), 1) + core * own
    )
    d_own = nn(low[...], pick.astype(f32).astype(bf16))
    grad = tn(d_own.astype(bf16), stacked[...]).T.reshape(64, 3 * d // 64, own)
    left = grad[:, :16]
    right = jnp.concatenate([grad[:, 16:], jnp.zeros((64, 8, own), f32)], axis=1)
    packed = jnp.concatenate([left, right], axis=2)

    d_sender = from_units(
        low[...], pl.ds(pl.multiple_of(d + core * half, half), half)
    ).astype(bf16)
    d_receiver = from_units(
        low[...], pl.ds(pl.multiple_of(2 * d + core * half, half), half)
    ).astype(bf16)
    table_grad = nn(onehot_columns(senders, n + h), d_sender)
    base[...] += table_grad[:n] + nn(back, d_receiver)
    outgoing[...] = jnp.concatenate(
        [
            table_grad[n:, :TILE].reshape(64, 8, TILE),
            table_grad[n:, TILE:].reshape(64, 8, TILE),
            packed,
        ],
        axis=1,
    ).astype(bf16)


def finish_kernel(incoming, base, send, node_grad, first_grad):
    values = incoming[...].astype(f32)
    rows = values.shape[0] * 8
    returned = jnp.concatenate(
        [values[:, :8].reshape(rows, TILE), values[:, 8:16].reshape(rows, TILE)], axis=1
    ).astype(bf16)
    hot = onehot_columns(flat_row(send[...]), base.shape[0])
    by_slot = tn(slot_order(*send.shape), returned).astype(bf16)
    node_grad[...] = (base[...] + nn(hot, by_slot)).astype(bf16)
    total = jnp.sum(values[:, 16:], axis=0)
    own = first_grad.shape[1]
    first_grad[...] = jnp.concatenate([total[:, :own], total[:8, own:]], axis=0)


def per_device(
    nodes,
    edges,
    node_cotangent,
    edge_first,
    edge_second,
    node_first,
    node_second,
    sender,
    receiver_pos,
    block_tile,
    live_blocks,
    send_rows,
):
    n, d = nodes.shape
    e = edges.shape[0]
    half = d // 2
    peers, slots = send_rows.shape[1], send_rows.shape[2]
    h = peers * slots
    columns = lax.axis_size("y")
    own = edge_second.shape[0]
    units = own * columns * lax.axis_size("core")
    width = edge_first.shape[0] + node_first.shape[0] + 2 * d
    vmem = pl.BlockSpec(memory_space=pltpu.VMEM)
    smem = pl.BlockSpec(memory_space=pltpu.SMEM)
    params = pltpu.CompilerParams(vmem_limit_bytes=VMEM_LIMIT)
    send = send_rows[0].T

    supply, shard = pl.pallas_call(
        supply_kernel,
        out_shape=(
            jax.ShapeDtypeStruct((h, half), bf16),
            jax.ShapeDtypeStruct((own, width), bf16),
        ),
        in_specs=[vmem] * 6,
        out_specs=(vmem, vmem),
        compiler_params=params,
        name="supply",
    )(nodes, send, edge_first.T, edge_second, node_first.T, node_second)
    pair = lax.all_gather(shard, "core", axis=0, tiled=True)
    beside = [
        (2 * i + c, 2 * ((i + (1, columns - 1)[c]) % columns) + c)
        for i in range(columns)
        for c in range(2)
    ]
    near = lax.ppermute(pair, ("y", "core"), beside)
    start = lax.axis_index("core") * own
    relayed = lax.dynamic_slice_in_dim(near, start, own, 0)
    far = lax.ppermute(relayed, ("y", "core"), beside)
    received = lax.all_to_all(
        supply.reshape(peers, slots, half), ("x", "z"), split_axis=0, concat_axis=0, tiled=True
    ).reshape(h, half)
    near_other = lax.ppermute(near, "core", [(0, 1), (1, 0)])
    far_other = lax.ppermute(far, "core", [(0, 1), (1, 0)])
    halo = lax.all_gather(received, "core", axis=0, tiled=True)

    node_out, outgoing, base = pl.pallas_call(
        step_kernel,
        out_shape=(
            jax.ShapeDtypeStruct((n, d), bf16),
            jax.ShapeDtypeStruct((peers, 32, TILE), bf16),
            jax.ShapeDtypeStruct((n, half), f32),
        ),
        in_specs=[smem, smem] + [vmem] * 11,
        out_specs=(vmem, vmem, vmem),
        scratch_shapes=[
            pltpu.VMEM((n + h, d), bf16),
            pltpu.VMEM((e, 3 * d), bf16),
            pltpu.VMEM((e, units), f32),
            pltpu.VMEM((e, units), f32),
            pltpu.VMEM((e, d), f32),
            pltpu.VMEM((e, TILE), f32),
            pltpu.VMEM((e, units), bf16),
            pltpu.VMEM((e, n), bf16),
            pltpu.VMEM((units, width), bf16),
        ],
        compiler_params=params,
        name="step",
    )(
        block_tile,
        live_blocks,
        nodes,
        edges,
        node_cotangent,
        halo,
        pair,
        near,
        far,
        near_other,
        far_other,
        sender.reshape(e // TILE, TILE),
        receiver_pos.reshape(e // TILE, TILE),
    )
    incoming = lax.all_to_all(outgoing, ("x", "z"), split_axis=0, concat_axis=0, tiled=True)
    half_grad, first_grad = pl.pallas_call(
        finish_kernel,
        out_shape=(
            jax.ShapeDtypeStruct((n, half), bf16),
            jax.ShapeDtypeStruct((edge_first.shape[0] // peers, own), f32),
        ),
        in_specs=[vmem] * 3,
        out_specs=(vmem, vmem),
        compiler_params=params,
        name="finish",
    )(incoming, base, send)
    node_grad = lax.all_gather(half_grad, "core", axis=1, tiled=True)
    return (node_out, node_grad, first_grad)


def solution(mesh):
    devices = mesh.devices
    tiles, shares = devices.shape
    fine = Mesh(devices.reshape(4, tiles // 4, shares // 2, 2), ("x", "z", "y", "core"))
    tile = ("x", "z")
    hid = ("y", "core")
    in_specs = (
        P(tile, None),
        P(tile, None),
        P(tile, None),
        P(None, hid),
        P(hid, None),
        P(None, hid),
        P(hid, None),
        P(tile),
        P(tile),
        P(tile),
        P(tile),
        P(tile, None, None),
    )
    out_specs = (P(tile, None), P(tile, None), P(tile, hid))
    return jax.shard_map(
        per_device, mesh=fine, in_specs=in_specs, out_specs=out_specs, check_vma=False
    )
```

```python
import jax
import jax.numpy as jnp
from jax import lax
from jax.experimental import pallas as pl
from jax.experimental.pallas import tpu as pltpu
from jax.sharding import Mesh, PartitionSpec as P

TILE = 128
epsilon = 1e-05
bf16 = jnp.bfloat16
f32 = jnp.float32
SUPPLY_VMEM = 60 * 1024 * 1024
STEP_VMEM = 24 * 1024 * 1024
FINISH_VMEM = 16 * 1024 * 1024
CHUNK = 32
BLOCK = 256


def nn(a, b):
    return lax.dot_general(a, b, (((1,), (0,)), ((), ())), preferred_element_type=f32)


def nt(a, b):
    return lax.dot_general(a, b, (((1,), (1,)), ((), ())), preferred_element_type=f32)


def tn(a, b):
    return lax.dot_general(a, b, (((0,), (0,)), ((), ())), preferred_element_type=f32)


def onehot_rows(index_row, count):
    n = index_row.shape[1]
    column = jnp.broadcast_to(index_row, (TILE, n)).T
    lanes = lax.broadcasted_iota(jnp.int32, (n, TILE), 1)
    return jnp.concatenate(
        [(column == lanes + k * TILE).astype(f32).astype(bf16) for k in range(count // TILE)],
        axis=1,
    )


def onehot_columns(index_row, count):
    n = index_row.shape[1]
    rows = lax.broadcasted_iota(jnp.int32, (count, n), 0)
    return (index_row == rows).astype(f32).astype(bf16)


def flat_row(rows):
    return jnp.concatenate([rows[i : i + 1] for i in range(rows.shape[0])], axis=1)


def slot_order(slots, peers):
    count = slots * peers
    row = lax.broadcasted_iota(jnp.int32, (count, count), 0)
    column = lax.broadcasted_iota(jnp.int32, (count, count), 1)
    return ((row % slots) * peers + row // slots == column).astype(f32).astype(bf16)


def supply_kernel(nodes, send, first, second, node_first, node_second, supply, weights):
    core = lax.axis_index("core")
    half = nodes.shape[1] // 2
    hot = onehot_rows(flat_row(send[...]), nodes.shape[0])
    columns = pl.ds(pl.multiple_of(core * half, half), half)
    rows = nn(hot, nodes[:, columns]).astype(bf16)
    supply[...] = nn(slot_order(*send.shape), rows).astype(bf16)
    at = 0
    for part in (first, node_first, second, node_second):
        weights[:, at : at + part.shape[1]] = part[...]
        at += part.shape[1]


def sigmoid(v):
    return 0.5 * jnp.tanh(0.5 * v) + 0.5


def normed(v):
    centre = jnp.mean(v, axis=-1, keepdims=True)
    shifted = v - centre
    variance = jnp.mean(shifted * shifted, axis=-1, keepdims=True)
    scale = lax.rsqrt(variance + epsilon)
    return shifted * scale, scale


def normed_back(g, unit, scale):
    return scale * (
        g
        - jnp.mean(g, axis=-1, keepdims=True)
        - unit * jnp.mean(g * unit, axis=-1, keepdims=True)
    )


def by_rows(start, body):
    for at in range(start, start + BLOCK, CHUNK):
        body(pl.ds(at, CHUNK))


def step_kernel(
    nodes,
    edges,
    cotangent,
    halo,
    pair,
    near,
    far,
    near_other,
    far_other,
    sender,
    receivers,
    node_out,
    outgoing,
    base,
    table,
    stacked,
    wide,
    slope,
    unit,
    scale,
    low,
    received,
    weights,
):
    d = nodes.shape[1]
    half = d // 2
    n = nodes.shape[0]
    e = edges.shape[0]
    h = halo.shape[0] // 2
    core = lax.axis_index("core")
    first = pl.ds(0, 3 * d)
    node_first = pl.ds(3 * d, 2 * d)
    second = pl.ds(5 * d, d)
    node_second = pl.ds(6 * d, d)
    parts = (pair, near, far, near_other, far_other)
    units = 0
    for piece in parts:
        weights[units : units + piece.shape[0], :] = piece[...]
        units += piece.shape[0]

    def to_units(x, columns):
        return nt(x, weights[:, columns])

    def from_units(x, columns):
        return nn(x, weights[:, columns])

    table[:n] = nodes[...]
    table[n:, :half] = halo[:h]
    table[n:, half:] = halo[h:]
    receiver = flat_row(receivers[...])
    received[...] = onehot_rows(receiver, n)
    senders = flat_row(sender[...])
    stacked[:, :d] = edges[...]
    stacked[:, d : 2 * d] = nn(onehot_rows(senders, n + h), table[...]).astype(bf16)
    stacked[:, 2 * d :] = nn(received[...], nodes[...]).astype(bf16)

    def activate(rows):
        v = wide[rows, :]
        s = sigmoid(v)
        low[rows, :] = (v * s).astype(bf16)
        slope[rows, :] = s * (1.0 + v * (1.0 - s))

    def normalise(rows):
        u, r = normed(wide[rows, :])
        unit[rows, :] = u
        scale[rows, :] = jnp.broadcast_to(r, (CHUNK, TILE))
        low[rows, :] = (edges[rows, :].astype(f32) + u).astype(bf16)

    def block(start):
        return pl.ds(start, BLOCK)

    starts = range(0, e, BLOCK)
    for at in starts:
        wide[block(at), :] = to_units(stacked[block(at), :], first)
        by_rows(at, activate)
    for at in starts:
        wide[block(at), :] = from_units(low[block(at), :], second)
        by_rows(at, normalise)
    back = onehot_columns(receiver, n)
    aggregated = nn(back, low[...]).astype(bf16)

    preact_node = to_units(jnp.concatenate([nodes[...], aggregated], axis=1), node_first)
    s = sigmoid(preact_node)
    hidden_node = (preact_node * s).astype(bf16)
    node_unit, node_scale = normed(from_units(hidden_node, node_second))
    node_out[...] = (nodes[...].astype(f32) + node_unit).astype(bf16)
    d_node_sum = normed_back(cotangent[...].astype(f32), node_unit, node_scale).astype(bf16)
    d_preact_node = (
        to_units(d_node_sum, node_second) * (s * (1.0 + preact_node * (1.0 - s)))
    ).astype(bf16)
    d_aggregated = from_units(d_preact_node, pl.ds(4 * d, d)).astype(bf16)
    columns = pl.ds(pl.multiple_of(core * half, half), half)
    base[...] = cotangent[:, columns].astype(f32) + from_units(
        d_preact_node, pl.ds(pl.multiple_of(3 * d + core * half, half), half)
    )

    def denormalise(rows):
        low[rows, :] = normed_back(wide[rows, :], unit[rows, :], scale[rows, :1]).astype(bf16)

    def deactivate(rows):
        low[rows, :] = (wide[rows, :] * slope[rows, :]).astype(bf16)

    for at in starts:
        wide[block(at), :] = nn(received[block(at), :], d_aggregated)
        by_rows(at, denormalise)
    for at in starts:
        wide[block(at), :] = to_units(low[block(at), :], second)
        by_rows(at, deactivate)

    own = units // 8
    pick = (
        lax.broadcasted_iota(jnp.int32, (units, own), 0)
        == lax.broadcasted_iota(jnp.int32, (units, own), 1) + core * own
    )
    d_own = nn(low[...], pick.astype(f32).astype(bf16))
    grad = tn(d_own.astype(bf16), stacked[...]).T.reshape(64, 3 * d // 64, own)
    left = grad[:, :16]
    right = jnp.concatenate([grad[:, 16:], jnp.zeros((64, 8, own), f32)], axis=1)
    packed = jnp.concatenate([left, right], axis=2)

    d_sender = from_units(
        low[...], pl.ds(pl.multiple_of(d + core * half, half), half)
    ).astype(bf16)
    d_receiver = from_units(
        low[...], pl.ds(pl.multiple_of(2 * d + core * half, half), half)
    ).astype(bf16)
    table_grad = nn(onehot_columns(senders, n + h), d_sender)
    base[...] += table_grad[:n] + nn(back, d_receiver)
    outgoing[...] = jnp.concatenate(
        [
            table_grad[n:, :TILE].reshape(64, 8, TILE),
            table_grad[n:, TILE:].reshape(64, 8, TILE),
            packed,
        ],
        axis=1,
    ).astype(bf16)


def run_step(
    nodes, edges, cotangent, halo, pair, near, far, near_other, far_other, sender, receivers
):
    n, d = nodes.shape
    e = edges.shape[0]
    h = halo.shape[0] // 2
    units = 4 * pair.shape[0]
    vmem = pl.BlockSpec(memory_space=pltpu.VMEM)
    return pl.pallas_call(
        step_kernel,
        out_shape=(
            jax.ShapeDtypeStruct((n, d), bf16),
            jax.ShapeDtypeStruct((64, 32, TILE), bf16),
            jax.ShapeDtypeStruct((n, d // 2), f32),
        ),
        in_specs=[vmem] * 11,
        out_specs=(vmem, vmem, vmem),
        scratch_shapes=[
            pltpu.VMEM((n + h, d), bf16),
            pltpu.VMEM((e, 3 * d), bf16),
            pltpu.VMEM((e, units), f32),
            pltpu.VMEM((e, units), f32),
            pltpu.VMEM((e, d), f32),
            pltpu.VMEM((e, TILE), f32),
            pltpu.VMEM((e, units), bf16),
            pltpu.VMEM((e, n), bf16),
            pltpu.VMEM((units, pair.shape[1]), bf16),
        ],
        compiler_params=pltpu.CompilerParams(vmem_limit_bytes=STEP_VMEM),
        name="step",
    )(nodes, edges, cotangent, halo, pair, near, far, near_other, far_other, sender, receivers)


def finish_kernel(incoming, base, send, node_grad, first_grad):
    values = incoming[...].astype(f32)
    rows = values.shape[0] * 8
    returned = jnp.concatenate(
        [values[:, :8].reshape(rows, TILE), values[:, 8:16].reshape(rows, TILE)], axis=1
    ).astype(bf16)
    hot = onehot_columns(flat_row(send[...]), base.shape[0])
    by_slot = tn(slot_order(*send.shape), returned).astype(bf16)
    node_grad[...] = (base[...] + nn(hot, by_slot)).astype(bf16)
    total = jnp.sum(values[:, 16:], axis=0)
    own = first_grad.shape[1]
    first_grad[...] = jnp.concatenate([total[:, :own], total[:8, own:]], axis=0)


def per_device(
    nodes,
    edges,
    node_cotangent,
    edge_first,
    edge_second,
    node_first,
    node_second,
    sender,
    receiver_pos,
    block_tile,
    live_blocks,
    send_rows,
):
    n, d = nodes.shape
    e = edges.shape[0]
    half = d // 2
    peers, slots = send_rows.shape[1], send_rows.shape[2]
    h = peers * slots
    columns = lax.axis_size("y")
    own = edge_second.shape[0]
    width = edge_first.shape[0] + node_first.shape[0] + 2 * d
    vmem = pl.BlockSpec(memory_space=pltpu.VMEM)
    send = send_rows[0].T

    supply, shard = pl.pallas_call(
        supply_kernel,
        out_shape=(
            jax.ShapeDtypeStruct((h, half), bf16),
            jax.ShapeDtypeStruct((own, width), bf16),
        ),
        in_specs=[vmem] * 6,
        out_specs=(vmem, vmem),
        compiler_params=pltpu.CompilerParams(vmem_limit_bytes=SUPPLY_VMEM),
        name="supply",
    )(nodes, send, edge_first.T, edge_second, node_first.T, node_second)
    pair = lax.all_gather(shard, "core", axis=0, tiled=True)
    beside = [
        (2 * i + c, 2 * ((i + (1, columns - 1)[c]) % columns) + c)
        for i in range(columns)
        for c in range(2)
    ]
    near = lax.ppermute(pair, ("y", "core"), beside)
    start = lax.axis_index("core") * own
    relayed = lax.dynamic_slice_in_dim(near, start, own, 0)
    far = lax.ppermute(relayed, ("y", "core"), beside)
    received = lax.all_to_all(
        supply.reshape(peers, slots, half), ("x", "z"), split_axis=0, concat_axis=0, tiled=True
    ).reshape(h, half)
    near_other = lax.ppermute(near, "core", [(0, 1), (1, 0)])
    far_other = lax.ppermute(far, "core", [(0, 1), (1, 0)])
    halo = lax.all_gather(received, "core", axis=0, tiled=True)

    blocks = block_tile.shape[0]
    receivers = jnp.where(
        jnp.arange(blocks, dtype=jnp.int32)[:, None] < live_blocks,
        receiver_pos.reshape(blocks, TILE) + block_tile[:, None] * TILE,
        -1,
    )
    node_out, outgoing, base = run_step(
        nodes,
        edges,
        node_cotangent,
        halo,
        pair,
        near,
        far,
        near_other,
        far_other,
        sender.reshape(blocks, TILE),
        receivers,
    )
    incoming = lax.all_to_all(outgoing, ("x", "z"), split_axis=0, concat_axis=0, tiled=True)
    half_grad, first_grad = pl.pallas_call(
        finish_kernel,
        out_shape=(
            jax.ShapeDtypeStruct((n, half), bf16),
            jax.ShapeDtypeStruct((edge_first.shape[0] // peers, own), f32),
        ),
        in_specs=[vmem] * 3,
        out_specs=(vmem, vmem),
        compiler_params=pltpu.CompilerParams(vmem_limit_bytes=FINISH_VMEM),
        name="finish",
    )(incoming, base, send)
    node_grad = lax.all_gather(half_grad, "core", axis=1, tiled=True)
    return (node_out, node_grad, first_grad)


def solution(mesh):
    devices = mesh.devices
    tiles, shares = devices.shape
    fine = Mesh(devices.reshape(4, tiles // 4, shares // 2, 2), ("x", "z", "y", "core"))
    tile = ("x", "z")
    hid = ("y", "core")
    in_specs = (
        P(tile, None),
        P(tile, None),
        P(tile, None),
        P(None, hid),
        P(hid, None),
        P(None, hid),
        P(hid, None),
        P(tile),
        P(tile),
        P(tile),
        P(tile),
        P(tile, None, None),
    )
    out_specs = (P(tile, None), P(tile, None), P(tile, hid))
    return jax.shard_map(
        per_device, mesh=fine, in_specs=in_specs, out_specs=out_specs, check_vma=False
    )
```

```python
import jax
import jax.numpy as jnp
from jax import lax
from jax.experimental import pallas as pl
from jax.experimental.pallas import tpu as pltpu
from jax.sharding import Mesh, PartitionSpec as P

TILE = 128
epsilon = 1e-05
bf16 = jnp.bfloat16
f32 = jnp.float32
SUPPLY_VMEM = 60 * 1024 * 1024
STEP_VMEM = 24 * 1024 * 1024
FINISH_VMEM = 16 * 1024 * 1024
CHUNK = 32
BLOCK = 256


def nn(a, b):
    return lax.dot_general(a, b, (((1,), (0,)), ((), ())), preferred_element_type=f32)


def nt(a, b):
    return lax.dot_general(a, b, (((1,), (1,)), ((), ())), preferred_element_type=f32)


def tn(a, b):
    return lax.dot_general(a, b, (((0,), (0,)), ((), ())), preferred_element_type=f32)


def onehot_rows(index_row, count):
    n = index_row.shape[1]
    column = jnp.broadcast_to(index_row, (TILE, n)).T
    lanes = lax.broadcasted_iota(jnp.int32, (n, TILE), 1)
    return jnp.concatenate(
        [(column == lanes + k * TILE).astype(f32).astype(bf16) for k in range(count // TILE)],
        axis=1,
    )


def onehot_columns(index_row, count):
    n = index_row.shape[1]
    rows = lax.broadcasted_iota(jnp.int32, (count, n), 0)
    return (index_row == rows).astype(f32).astype(bf16)


def flat_row(rows):
    return jnp.concatenate([rows[i : i + 1] for i in range(rows.shape[0])], axis=1)


def slot_order(slots, peers):
    count = slots * peers
    row = lax.broadcasted_iota(jnp.int32, (count, count), 0)
    column = lax.broadcasted_iota(jnp.int32, (count, count), 1)
    return ((row % slots) * peers + row // slots == column).astype(f32).astype(bf16)


def supply_kernel(nodes, send, first, second, node_first, node_second, supply, weights):
    core = lax.axis_index("core")
    half = nodes.shape[1] // 2
    hot = onehot_rows(flat_row(send[...]), nodes.shape[0])
    columns = pl.ds(pl.multiple_of(core * half, half), half)
    rows = nn(hot, nodes[:, columns]).astype(bf16)
    supply[...] = nn(slot_order(*send.shape), rows).astype(bf16)
    at = 0
    for part in (first, node_first, second, node_second):
        weights[:, at : at + part.shape[1]] = part[...]
        at += part.shape[1]


def sigmoid(v):
    return 0.5 * jnp.tanh(0.5 * v) + 0.5


def normed(v):
    centre = jnp.mean(v, axis=-1, keepdims=True)
    shifted = v - centre
    variance = jnp.mean(shifted * shifted, axis=-1, keepdims=True)
    scale = lax.rsqrt(variance + epsilon)
    return shifted * scale, scale


def normed_back(g, unit, scale):
    return scale * (
        g
        - jnp.mean(g, axis=-1, keepdims=True)
        - unit * jnp.mean(g * unit, axis=-1, keepdims=True)
    )


def by_rows(start, body):
    for at in range(start, start + BLOCK, CHUNK):
        body(pl.ds(at, CHUNK))


def step_kernel(
    nodes,
    edges,
    cotangent,
    halo,
    pair,
    near,
    far,
    near_other,
    far_other,
    sender,
    receivers,
    node_out,
    outgoing,
    base,
    table,
    stacked,
    wide,
    slope,
    unit,
    scale,
    low,
    received,
    weights,
):
    d = nodes.shape[1]
    half = d // 2
    n = nodes.shape[0]
    e = edges.shape[0]
    h = halo.shape[0] // 2
    core = lax.axis_index("core")
    first = pl.ds(0, 3 * d)
    node_first = pl.ds(3 * d, 2 * d)
    second = pl.ds(5 * d, d)
    node_second = pl.ds(6 * d, d)
    parts = (pair, near, far, near_other, far_other)
    units = 0
    for piece in parts:
        weights[units : units + piece.shape[0], :] = piece[...]
        units += piece.shape[0]

    def to_units(x, columns):
        return nt(x, weights[:, columns])

    def from_units(x, columns):
        return nn(x, weights[:, columns])

    table[:n] = nodes[...]
    table[n:, :half] = halo[:h]
    table[n:, half:] = halo[h:]
    receiver = flat_row(receivers[...])
    received[...] = onehot_rows(receiver, n)
    senders = flat_row(sender[...])
    stacked[:, :d] = edges[...]
    stacked[:, d : 2 * d] = nn(onehot_rows(senders, n + h), table[...]).astype(bf16)
    stacked[:, 2 * d :] = nn(received[...], nodes[...]).astype(bf16)

    def activate(rows):
        v = wide[rows, :]
        s = sigmoid(v)
        low[rows, :] = (v * s).astype(bf16)
        slope[rows, :] = s * (1.0 + v * (1.0 - s))

    def normalise(rows):
        u, r = normed(wide[rows, :])
        unit[rows, :] = u
        scale[rows, :] = jnp.broadcast_to(r, (CHUNK, TILE))
        low[rows, :] = (edges[rows, :].astype(f32) + u).astype(bf16)

    def block(start):
        return pl.ds(start, BLOCK)

    starts = range(0, e, BLOCK)
    for at in starts:
        wide[block(at), :] = to_units(stacked[block(at), :], first)
        by_rows(at, activate)
    for at in starts:
        wide[block(at), :] = from_units(low[block(at), :], second)
        by_rows(at, normalise)
    back = onehot_columns(receiver, n)
    aggregated = nn(back, low[...]).astype(bf16)

    preact_node = to_units(jnp.concatenate([nodes[...], aggregated], axis=1), node_first)
    s = sigmoid(preact_node)
    hidden_node = (preact_node * s).astype(bf16)
    node_unit, node_scale = normed(from_units(hidden_node, node_second))
    node_out[...] = (nodes[...].astype(f32) + node_unit).astype(bf16)
    d_node_sum = normed_back(cotangent[...].astype(f32), node_unit, node_scale).astype(bf16)
    d_preact_node = (
        to_units(d_node_sum, node_second) * (s * (1.0 + preact_node * (1.0 - s)))
    ).astype(bf16)
    d_aggregated = from_units(d_preact_node, pl.ds(4 * d, d)).astype(bf16)
    own = units // 8
    lane = pl.multiple_of(lax.axis_index("y") * TILE, TILE)
    direct = cotangent[:, pl.ds(lane, TILE)].astype(f32) + from_units(
        d_preact_node, pl.ds(3 * d + lane, TILE)
    )
    direct = jnp.where(core == 0, direct[:, :own], direct[:, own : 2 * own])

    def denormalise(rows):
        low[rows, :] = normed_back(wide[rows, :], unit[rows, :], scale[rows, :1]).astype(bf16)

    def deactivate(rows):
        low[rows, :] = (wide[rows, :] * slope[rows, :]).astype(bf16)

    for at in starts:
        wide[block(at), :] = nn(received[block(at), :], d_aggregated)
        by_rows(at, denormalise)
    for at in starts:
        wide[block(at), :] = to_units(low[block(at), :], second)
        by_rows(at, deactivate)

    pick = (
        lax.broadcasted_iota(jnp.int32, (units, own), 0)
        == lax.broadcasted_iota(jnp.int32, (units, own), 1) + core * own
    )
    d_own = nn(low[...], pick.astype(f32).astype(bf16))
    grad = tn(d_own.astype(bf16), stacked[...]).T.reshape(64, 3 * d // 64, own)
    left = grad[:, :16]
    right = jnp.concatenate([grad[:, 16:], jnp.zeros((64, 8, own), f32)], axis=1)
    packed = jnp.concatenate([left, right], axis=2)

    d_sender = from_units(low[...], pl.ds(d + lane, TILE)).astype(bf16)
    d_receiver = from_units(low[...], pl.ds(2 * d + lane, TILE)).astype(bf16)
    table_grad = nn(onehot_columns(senders, n + h), d_sender)
    table_grad = jnp.where(core == 0, table_grad[:, :own], table_grad[:, own : 2 * own])
    receiver_grad = nn(back, d_receiver)
    base[...] = direct + table_grad[:n] + jnp.where(
        core == 0, receiver_grad[:, :own], receiver_grad[:, own : 2 * own]
    )
    d_own = jnp.where(core == 0, low[:, :own], low[:, own : 2 * own])
    grad = tn(d_own, stacked[...]).T.reshape(64, 3 * d // 64, own)
    both = jnp.concatenate([table_grad[n:].reshape(64, 8, own), grad], axis=1)
    outgoing[...] = jnp.concatenate([both[:, :16], both[:, 16:]], axis=2).astype(bf16)


def run_step(
    nodes, edges, cotangent, halo, pair, near, far, near_other, far_other, sender, receivers
):
    n, d = nodes.shape
    e = edges.shape[0]
    h = halo.shape[0] // 2
    units = 4 * pair.shape[0]
    vmem = pl.BlockSpec(memory_space=pltpu.VMEM)
    return pl.pallas_call(
        step_kernel,
        out_shape=(
            jax.ShapeDtypeStruct((n, d), bf16),
            jax.ShapeDtypeStruct((64, 16, TILE), bf16),
            jax.ShapeDtypeStruct((n, d // 8), f32),
        ),
        in_specs=[vmem] * 11,
        out_specs=(vmem, vmem, vmem),
        scratch_shapes=[
            pltpu.VMEM((n + h, d), bf16),
            pltpu.VMEM((e, 3 * d), bf16),
            pltpu.VMEM((e, units), f32),
            pltpu.VMEM((e, units), f32),
            pltpu.VMEM((e, d), f32),
            pltpu.VMEM((e, TILE), f32),
            pltpu.VMEM((e, units), bf16),
            pltpu.VMEM((e, n), bf16),
            pltpu.VMEM((units, pair.shape[1]), bf16),
        ],
        compiler_params=pltpu.CompilerParams(vmem_limit_bytes=STEP_VMEM),
        name="step",
    )(nodes, edges, cotangent, halo, pair, near, far, near_other, far_other, sender, receivers)


def finish_kernel(incoming, base, send, node_grad, first_grad):
    values = incoming[...].astype(f32)
    own = first_grad.shape[1]
    returned = values[:, :8, :own].reshape(values.shape[0] * 8, own).astype(bf16)
    hot = onehot_columns(flat_row(send[...]), base.shape[0])
    by_slot = tn(slot_order(*send.shape), returned).astype(bf16)
    part = (base[...] + nn(hot, by_slot)).astype(bf16)
    packed = jnp.concatenate([part[:TILE], part[TILE:]], axis=1)
    for share in range(node_grad.shape[0]):
        node_grad[share] = packed
    total = jnp.sum(values, axis=0)
    first_grad[...] = jnp.concatenate([total[8:, :own], total[:, own:]], axis=0)


def place_kernel(parts, node_grad):
    own = parts.shape[2] // 2
    for pair in range(parts.shape[0] // 2):
        low, high = parts[2 * pair], parts[2 * pair + 1]
        columns = pl.ds(pair * TILE, TILE)
        node_grad[:TILE, columns] = jnp.concatenate([low[:, :own], high[:, :own]], axis=1)
        node_grad[TILE:, columns] = jnp.concatenate([low[:, own:], high[:, own:]], axis=1)


def per_device(
    nodes,
    edges,
    node_cotangent,
    edge_first,
    edge_second,
    node_first,
    node_second,
    sender,
    receiver_pos,
    block_tile,
    live_blocks,
    send_rows,
):
    n, d = nodes.shape
    e = edges.shape[0]
    half = d // 2
    peers, slots = send_rows.shape[1], send_rows.shape[2]
    h = peers * slots
    columns = lax.axis_size("y")
    own = edge_second.shape[0]
    width = edge_first.shape[0] + node_first.shape[0] + 2 * d
    vmem = pl.BlockSpec(memory_space=pltpu.VMEM)
    send = send_rows[0].T

    supply, shard = pl.pallas_call(
        supply_kernel,
        out_shape=(
            jax.ShapeDtypeStruct((h, half), bf16),
            jax.ShapeDtypeStruct((own, width), bf16),
        ),
        in_specs=[vmem] * 6,
        out_specs=(vmem, vmem),
        compiler_params=pltpu.CompilerParams(vmem_limit_bytes=SUPPLY_VMEM),
        name="supply",
    )(nodes, send, edge_first.T, edge_second, node_first.T, node_second)
    pair = lax.all_gather(shard, "core", axis=0, tiled=True)
    beside = [
        (2 * i + c, 2 * ((i + (1, columns - 1)[c]) % columns) + c)
        for i in range(columns)
        for c in range(2)
    ]
    near = lax.ppermute(pair, ("y", "core"), beside)
    start = lax.axis_index("core") * own
    relayed = lax.dynamic_slice_in_dim(near, start, own, 0)
    far = lax.ppermute(relayed, ("y", "core"), beside)
    received = lax.all_to_all(
        supply.reshape(peers, slots, half), ("x", "z"), split_axis=0, concat_axis=0, tiled=True
    ).reshape(h, half)
    near_other = lax.ppermute(near, "core", [(0, 1), (1, 0)])
    far_other = lax.ppermute(far, "core", [(0, 1), (1, 0)])
    halo = lax.all_gather(received, "core", axis=0, tiled=True)

    blocks = block_tile.shape[0]
    receivers = jnp.where(
        jnp.arange(blocks, dtype=jnp.int32)[:, None] < live_blocks,
        receiver_pos.reshape(blocks, TILE) + block_tile[:, None] * TILE,
        -1,
    )
    node_out, outgoing, base = run_step(
        nodes,
        edges,
        node_cotangent,
        halo,
        pair,
        near,
        far,
        near_other,
        far_other,
        sender.reshape(blocks, TILE),
        receivers,
    )
    incoming = lax.all_to_all(outgoing, ("x", "z"), split_axis=0, concat_axis=0, tiled=True)
    copies, first_grad = pl.pallas_call(
        finish_kernel,
        out_shape=(
            jax.ShapeDtypeStruct((2 * columns, TILE, TILE), bf16),
            jax.ShapeDtypeStruct((edge_first.shape[0] // peers, own), f32),
        ),
        in_specs=[vmem] * 3,
        out_specs=(vmem, vmem),
        compiler_params=pltpu.CompilerParams(vmem_limit_bytes=FINISH_VMEM),
        name="finish",
    )(incoming, base, send)
    parts = lax.all_to_all(copies, ("y", "core"), split_axis=0, concat_axis=0, tiled=True)
    node_grad = pl.pallas_call(
        place_kernel,
        out_shape=jax.ShapeDtypeStruct((n, d), bf16),
        in_specs=[vmem],
        out_specs=vmem,
        compiler_params=pltpu.CompilerParams(vmem_limit_bytes=FINISH_VMEM),
        name="place",
    )(parts)
    return (node_out, node_grad, first_grad)


def solution(mesh):
    devices = mesh.devices
    tiles, shares = devices.shape
    fine = Mesh(devices.reshape(4, tiles // 4, shares // 2, 2), ("x", "z", "y", "core"))
    tile = ("x", "z")
    hid = ("y", "core")
    in_specs = (
        P(tile, None),
        P(tile, None),
        P(tile, None),
        P(None, hid),
        P(hid, None),
        P(None, hid),
        P(hid, None),
        P(tile),
        P(tile),
        P(tile),
        P(tile),
        P(tile, None, None),
    )
    out_specs = (P(tile, None), P(tile, None), P(tile, hid))
    return jax.shard_map(
        per_device, mesh=fine, in_specs=in_specs, out_specs=out_specs, check_vma=False
    )
```

```python
import jax
import jax.numpy as jnp
from jax import lax
from jax.experimental import pallas as pl
from jax.experimental.pallas import tpu as pltpu
from jax.sharding import Mesh, PartitionSpec as P

TILE = 128
epsilon = 1e-05
bf16 = jnp.bfloat16
f32 = jnp.float32
SUPPLY_VMEM = 60 * 1024 * 1024
STEP_VMEM = 24 * 1024 * 1024
FINISH_VMEM = 16 * 1024 * 1024
CHUNK = 32
BLOCK = 256


def nn(a, b):
    return lax.dot_general(a, b, (((1,), (0,)), ((), ())), preferred_element_type=f32)


def nt(a, b):
    return lax.dot_general(a, b, (((1,), (1,)), ((), ())), preferred_element_type=f32)


def tn(a, b):
    return lax.dot_general(a, b, (((0,), (0,)), ((), ())), preferred_element_type=f32)


def onehot_rows(index_row, count):
    n = index_row.shape[1]
    column = jnp.broadcast_to(index_row, (TILE, n)).T
    lanes = lax.broadcasted_iota(jnp.int32, (n, TILE), 1)
    return jnp.concatenate(
        [(column == lanes + k * TILE).astype(f32).astype(bf16) for k in range(count // TILE)],
        axis=1,
    )


def onehot_columns(index_row, count):
    n = index_row.shape[1]
    rows = lax.broadcasted_iota(jnp.int32, (count, n), 0)
    return (index_row == rows).astype(f32).astype(bf16)


def flat_row(rows):
    return jnp.concatenate([rows[i : i + 1] for i in range(rows.shape[0])], axis=1)


def slot_order(slots, peers):
    count = slots * peers
    row = lax.broadcasted_iota(jnp.int32, (count, count), 0)
    column = lax.broadcasted_iota(jnp.int32, (count, count), 1)
    return ((row % slots) * peers + row // slots == column).astype(f32).astype(bf16)


def supply_kernel(nodes, send, first, second, node_first, node_second, supply, weights):
    core = lax.axis_index("core")
    half = nodes.shape[1] // 2
    hot = onehot_rows(flat_row(send[...]), nodes.shape[0])
    columns = pl.ds(pl.multiple_of(core * half, half), half)
    rows = nn(hot, nodes[:, columns]).astype(bf16)
    supply[...] = nn(slot_order(*send.shape), rows).astype(bf16)
    at = 0
    for part in (first, node_first, second, node_second):
        weights[:, at : at + part.shape[1]] = part[...]
        at += part.shape[1]


def sigmoid(v):
    return 0.5 * jnp.tanh(0.5 * v) + 0.5


def normed(v):
    centre = jnp.mean(v, axis=-1, keepdims=True)
    shifted = v - centre
    variance = jnp.mean(shifted * shifted, axis=-1, keepdims=True)
    scale = lax.rsqrt(variance + epsilon)
    return shifted * scale, scale


def normed_back(g, unit, scale):
    return scale * (
        g
        - jnp.mean(g, axis=-1, keepdims=True)
        - unit * jnp.mean(g * unit, axis=-1, keepdims=True)
    )


def by_rows(start, body):
    for at in range(start, start + BLOCK, CHUNK):
        body(pl.ds(at, CHUNK))


def step_kernel(
    nodes,
    edges,
    cotangent,
    halo,
    pair,
    near,
    near_other,
    fars,
    sender,
    receivers,
    node_out,
    outgoing,
    base,
    table,
    stacked,
    wide,
    slope,
    unit,
    scale,
    low,
    received,
    weights,
):
    d = nodes.shape[1]
    half = d // 2
    n = nodes.shape[0]
    e = edges.shape[0]
    h = halo.shape[0] // 2
    core = lax.axis_index("core")
    first = pl.ds(0, 3 * d)
    node_first = pl.ds(3 * d, 2 * d)
    second = pl.ds(5 * d, d)
    node_second = pl.ds(6 * d, d)
    parts = (pair, near, near_other, fars)
    units = 0
    for piece in parts:
        weights[units : units + piece.shape[0], :] = piece[...]
        units += piece.shape[0]

    def to_units(x, columns):
        return nt(x, weights[:, columns])

    def from_units(x, columns):
        return nn(x, weights[:, columns])

    table[:n] = nodes[...]
    table[n:, :half] = halo[:h]
    table[n:, half:] = halo[h:]
    receiver = flat_row(receivers[...])
    received[...] = onehot_rows(receiver, n)
    senders = flat_row(sender[...])
    stacked[:, :d] = edges[...]
    stacked[:, d : 2 * d] = nn(onehot_rows(senders, n + h), table[...]).astype(bf16)
    stacked[:, 2 * d :] = nn(received[...], nodes[...]).astype(bf16)

    def activate(rows):
        v = wide[rows, :]
        s = sigmoid(v)
        low[rows, :] = (v * s).astype(bf16)
        slope[rows, :] = s * (1.0 + v * (1.0 - s))

    def normalise(rows):
        u, r = normed(wide[rows, :])
        unit[rows, :] = u
        scale[rows, :] = jnp.broadcast_to(r, (CHUNK, TILE))
        low[rows, :] = (edges[rows, :].astype(f32) + u).astype(bf16)

    def block(start):
        return pl.ds(start, BLOCK)

    starts = range(0, e, BLOCK)
    for at in starts:
        wide[block(at), :] = to_units(stacked[block(at), :], first)
        by_rows(at, activate)
    for at in starts:
        wide[block(at), :] = from_units(low[block(at), :], second)
        by_rows(at, normalise)
    back = onehot_columns(receiver, n)
    aggregated = nn(back, low[...]).astype(bf16)

    preact_node = to_units(jnp.concatenate([nodes[...], aggregated], axis=1), node_first)
    s = sigmoid(preact_node)
    hidden_node = (preact_node * s).astype(bf16)
    node_unit, node_scale = normed(from_units(hidden_node, node_second))
    node_out[...] = (nodes[...].astype(f32) + node_unit).astype(bf16)
    d_node_sum = normed_back(cotangent[...].astype(f32), node_unit, node_scale).astype(bf16)
    d_preact_node = (
        to_units(d_node_sum, node_second) * (s * (1.0 + preact_node * (1.0 - s)))
    ).astype(bf16)
    d_aggregated = from_units(d_preact_node, pl.ds(4 * d, d)).astype(bf16)
    own = units // 8
    lane = pl.multiple_of(lax.axis_index("y") * TILE, TILE)
    direct = cotangent[:, pl.ds(lane, TILE)].astype(f32) + from_units(
        d_preact_node, pl.ds(3 * d + lane, TILE)
    )
    direct = jnp.where(core == 0, direct[:, :own], direct[:, own : 2 * own])

    def denormalise(rows):
        low[rows, :] = normed_back(wide[rows, :], unit[rows, :], scale[rows, :1]).astype(bf16)

    def deactivate(rows):
        low[rows, :] = (wide[rows, :] * slope[rows, :]).astype(bf16)

    for at in starts:
        wide[block(at), :] = nn(received[block(at), :], d_aggregated)
        by_rows(at, denormalise)
    for at in starts:
        wide[block(at), :] = to_units(low[block(at), :], second)
        by_rows(at, deactivate)

    tails = jnp.concatenate(
        [weights[:, pl.ds(d + lane, TILE)], weights[:, pl.ds(2 * d + lane, TILE)]], axis=1
    )
    d_tails = nn(low[...], tails).astype(bf16)
    d_sender, d_receiver = d_tails[:, :TILE], d_tails[:, TILE:]
    table_grad = nn(onehot_columns(senders, n + h), d_sender)
    table_grad = jnp.where(core == 0, table_grad[:, :own], table_grad[:, own : 2 * own])
    receiver_grad = nn(back, d_receiver)
    base[...] = direct + table_grad[:n] + jnp.where(
        core == 0, receiver_grad[:, :own], receiver_grad[:, own : 2 * own]
    )
    d_own = jnp.where(core == 0, low[:, :own], low[:, own : 2 * own])
    grad = tn(d_own, stacked[...]).T.reshape(64, 3 * d // 64, own)
    both = jnp.concatenate([table_grad[n:].reshape(64, 8, own), grad], axis=1)
    outgoing[...] = jnp.concatenate([both[:, :16], both[:, 16:]], axis=2).astype(bf16)


def run_step(
    nodes, edges, cotangent, halo, pair, near, near_other, fars, sender, receivers
):
    n, d = nodes.shape
    e = edges.shape[0]
    h = halo.shape[0] // 2
    units = 4 * pair.shape[0]
    vmem = pl.BlockSpec(memory_space=pltpu.VMEM)
    return pl.pallas_call(
        step_kernel,
        out_shape=(
            jax.ShapeDtypeStruct((n, d), bf16),
            jax.ShapeDtypeStruct((64, 16, TILE), bf16),
            jax.ShapeDtypeStruct((n, d // 8), f32),
        ),
        in_specs=[vmem] * 10,
        out_specs=(vmem, vmem, vmem),
        scratch_shapes=[
            pltpu.VMEM((n + h, d), bf16),
            pltpu.VMEM((e, 3 * d), bf16),
            pltpu.VMEM((e, units), f32),
            pltpu.VMEM((e, units), f32),
            pltpu.VMEM((e, d), f32),
            pltpu.VMEM((e, TILE), f32),
            pltpu.VMEM((e, units), bf16),
            pltpu.VMEM((e, n), bf16),
            pltpu.VMEM((units, pair.shape[1]), bf16),
        ],
        compiler_params=pltpu.CompilerParams(vmem_limit_bytes=STEP_VMEM),
        name="step",
    )(nodes, edges, cotangent, halo, pair, near, near_other, fars, sender, receivers)


def finish_kernel(incoming, base, send, node_grad, first_grad):
    values = incoming[...].astype(f32)
    own = first_grad.shape[1]
    returned = values[:, :8, :own].reshape(values.shape[0] * 8, own).astype(bf16)
    hot = onehot_columns(flat_row(send[...]), base.shape[0])
    by_slot = tn(slot_order(*send.shape), returned).astype(bf16)
    part = (base[...] + nn(hot, by_slot)).astype(bf16)
    packed = jnp.concatenate([part[:TILE], part[TILE:]], axis=1)
    for share in range(node_grad.shape[0]):
        node_grad[share] = packed
    total = jnp.sum(values, axis=0)
    first_grad[...] = jnp.concatenate([total[8:, :own], total[:, own:]], axis=0)


def place_kernel(parts, node_grad):
    own = parts.shape[2] // 2
    for pair in range(parts.shape[0] // 2):
        low, high = parts[2 * pair], parts[2 * pair + 1]
        columns = pl.ds(pair * TILE, TILE)
        node_grad[:TILE, columns] = jnp.concatenate([low[:, :own], high[:, :own]], axis=1)
        node_grad[TILE:, columns] = jnp.concatenate([low[:, own:], high[:, own:]], axis=1)


def per_device(
    nodes,
    edges,
    node_cotangent,
    edge_first,
    edge_second,
    node_first,
    node_second,
    sender,
    receiver_pos,
    block_tile,
    live_blocks,
    send_rows,
):
    n, d = nodes.shape
    e = edges.shape[0]
    half = d // 2
    peers, slots = send_rows.shape[1], send_rows.shape[2]
    h = peers * slots
    columns = lax.axis_size("y")
    own = edge_second.shape[0]
    width = edge_first.shape[0] + node_first.shape[0] + 2 * d
    vmem = pl.BlockSpec(memory_space=pltpu.VMEM)
    send = send_rows[0].T

    supply, shard = pl.pallas_call(
        supply_kernel,
        out_shape=(
            jax.ShapeDtypeStruct((h, half), bf16),
            jax.ShapeDtypeStruct((own, width), bf16),
        ),
        in_specs=[vmem] * 6,
        out_specs=(vmem, vmem),
        compiler_params=pltpu.CompilerParams(vmem_limit_bytes=SUPPLY_VMEM),
        name="supply",
    )(nodes, send, edge_first.T, edge_second, node_first.T, node_second)
    pair = lax.all_gather(shard, "core", axis=0, tiled=True)
    beside = [
        (2 * i + c, 2 * ((i + (1, columns - 1)[c]) % columns) + c)
        for i in range(columns)
        for c in range(2)
    ]
    near = lax.ppermute(pair, ("y", "core"), beside)
    fars = lax.ppermute(near, ("y", "core"), beside)
    received = lax.all_to_all(
        supply.reshape(peers, slots, half), ("x", "z"), split_axis=0, concat_axis=0, tiled=True
    ).reshape(h, half)
    near_other = lax.ppermute(near, "core", [(0, 1), (1, 0)])
    halo = lax.all_gather(received, "core", axis=0, tiled=True)

    blocks = block_tile.shape[0]
    receivers = jnp.where(
        jnp.arange(blocks, dtype=jnp.int32)[:, None] < live_blocks,
        receiver_pos.reshape(blocks, TILE) + block_tile[:, None] * TILE,
        -1,
    )
    node_out, outgoing, base = run_step(
        nodes,
        edges,
        node_cotangent,
        halo,
        pair,
        near,
        near_other,
        fars,
        sender.reshape(blocks, TILE),
        receivers,
    )
    incoming = lax.all_to_all(outgoing, ("x", "z"), split_axis=0, concat_axis=0, tiled=True)
    copies, first_grad = pl.pallas_call(
        finish_kernel,
        out_shape=(
            jax.ShapeDtypeStruct((2 * columns, TILE, TILE), bf16),
            jax.ShapeDtypeStruct((edge_first.shape[0] // peers, own), f32),
        ),
        in_specs=[vmem] * 3,
        out_specs=(vmem, vmem),
        compiler_params=pltpu.CompilerParams(vmem_limit_bytes=FINISH_VMEM),
        name="finish",
    )(incoming, base, send)
    parts = lax.all_to_all(copies, ("y", "core"), split_axis=0, concat_axis=0, tiled=True)
    node_grad = pl.pallas_call(
        place_kernel,
        out_shape=jax.ShapeDtypeStruct((n, d), bf16),
        in_specs=[vmem],
        out_specs=vmem,
        compiler_params=pltpu.CompilerParams(vmem_limit_bytes=FINISH_VMEM),
        name="place",
    )(parts)
    return (node_out, node_grad, first_grad)


def solution(mesh):
    devices = mesh.devices
    tiles, shares = devices.shape
    fine = Mesh(devices.reshape(4, tiles // 4, shares // 2, 2), ("x", "z", "y", "core"))
    tile = ("x", "z")
    hid = ("y", "core")
    in_specs = (
        P(tile, None),
        P(tile, None),
        P(tile, None),
        P(None, hid),
        P(hid, None),
        P(None, hid),
        P(hid, None),
        P(tile),
        P(tile),
        P(tile),
        P(tile),
        P(tile, None, None),
    )
    out_specs = (P(tile, None), P(tile, None), P(tile, hid))
    return jax.shard_map(
        per_device, mesh=fine, in_specs=in_specs, out_specs=out_specs, check_vma=False
    )
```

```python
import jax
import jax.numpy as jnp
from jax import lax
from jax.experimental import pallas as pl
from jax.experimental.pallas import tpu as pltpu
from jax.sharding import Mesh, PartitionSpec as P

TILE = 128
epsilon = 1e-05
bf16 = jnp.bfloat16
f32 = jnp.float32
SUPPLY_VMEM = 60 * 1024 * 1024
STEP_VMEM = 24 * 1024 * 1024
FINISH_VMEM = 16 * 1024 * 1024
CHUNK = 32
BLOCK = 256


def nn(a, b):
    return lax.dot_general(a, b, (((1,), (0,)), ((), ())), preferred_element_type=f32)


def nt(a, b):
    return lax.dot_general(a, b, (((1,), (1,)), ((), ())), preferred_element_type=f32)


def tn(a, b):
    return lax.dot_general(a, b, (((0,), (0,)), ((), ())), preferred_element_type=f32)


def onehot_rows(index_row, count):
    n = index_row.shape[1]
    column = jnp.broadcast_to(index_row, (TILE, n)).T
    lanes = lax.broadcasted_iota(jnp.int32, (n, TILE), 1)
    return jnp.concatenate(
        [(column == lanes + k * TILE).astype(f32).astype(bf16) for k in range(count // TILE)],
        axis=1,
    )


def onehot_columns(index_row, count):
    n = index_row.shape[1]
    rows = lax.broadcasted_iota(jnp.int32, (count, n), 0)
    return (index_row == rows).astype(f32).astype(bf16)


def flat_row(rows):
    return jnp.concatenate([rows[i : i + 1] for i in range(rows.shape[0])], axis=1)


def slot_order(slots, peers):
    count = slots * peers
    row = lax.broadcasted_iota(jnp.int32, (count, count), 0)
    column = lax.broadcasted_iota(jnp.int32, (count, count), 1)
    return ((row % slots) * peers + row // slots == column).astype(f32).astype(bf16)


def supply_kernel(nodes, send, first, second, node_first, node_second, supply, weights):
    core = lax.axis_index("core")
    half = nodes.shape[1] // 2
    hot = onehot_rows(flat_row(send[...]), nodes.shape[0])
    columns = pl.ds(pl.multiple_of(core * half, half), half)
    rows = nn(hot, nodes[:, columns]).astype(bf16)
    supply[...] = nn(slot_order(*send.shape), rows).astype(bf16)
    at = 0
    for part in (first, node_first, second, node_second):
        weights[:, at : at + part.shape[1]] = part[...]
        at += part.shape[1]


def sigmoid(v):
    return 0.5 * jnp.tanh(0.5 * v) + 0.5


def normed(v):
    centre = jnp.mean(v, axis=-1, keepdims=True)
    shifted = v - centre
    variance = jnp.mean(shifted * shifted, axis=-1, keepdims=True)
    scale = lax.rsqrt(variance + epsilon)
    return shifted * scale, scale


def normed_back(g, unit, scale):
    return scale * (
        g
        - jnp.mean(g, axis=-1, keepdims=True)
        - unit * jnp.mean(g * unit, axis=-1, keepdims=True)
    )


def by_rows(start, body):
    for at in range(start, start + BLOCK, CHUNK):
        body(pl.ds(at, CHUNK))


def step_kernel(
    nodes,
    edges,
    cotangent,
    halo,
    pair,
    near,
    near_other,
    fars,
    sender,
    receivers,
    node_out,
    outgoing,
    base,
    table,
    stacked,
    wide,
    slope,
    unit,
    scale,
    low,
    received,
    weights,
    fresh,
    sems,
):
    d = nodes.shape[1]
    half = d // 2
    n = nodes.shape[0]
    e = edges.shape[0]
    h = halo.shape[0] // 2
    core = lax.axis_index("core")
    first = pl.ds(0, 3 * d)
    node_first = pl.ds(3 * d, 2 * d)
    second = pl.ds(5 * d, d)
    node_second = pl.ds(6 * d, d)
    units = 4 * pair.shape[0]
    late = [
        pltpu.make_async_copy(
            near_other.at[:, columns],
            weights.at[pl.ds(units - pair.shape[0], pair.shape[0]), columns],
            sems.at[i],
        )
        for i, columns in enumerate((first, pl.ds(3 * d, 4 * d)))
    ]
    for copy in late:
        copy.start()
    for i, piece in enumerate((pair, near, fars)):
        weights[i * piece.shape[0] : (i + 1) * piece.shape[0], :] = piece[...]

    def to_units(x, columns):
        return nt(x, weights[:, columns])

    def from_units(x, columns):
        return nn(x, weights[:, columns])

    table[:n] = nodes[...]
    table[n:, :half] = halo[:h]
    table[n:, half:] = halo[h:]
    receiver = flat_row(receivers[...])
    received[...] = onehot_rows(receiver, n)
    senders = flat_row(sender[...])
    stacked[:, :d] = edges[...]
    stacked[:, d : 2 * d] = nn(onehot_rows(senders, n + h), table[...]).astype(bf16)
    stacked[:, 2 * d :] = nn(received[...], nodes[...]).astype(bf16)

    def activate(rows):
        v = wide[rows, :]
        s = sigmoid(v)
        low[rows, :] = (v * s).astype(bf16)
        slope[rows, :] = s * (1.0 + v * (1.0 - s))

    def normalise(rows):
        u, r = normed(wide[rows, :])
        unit[rows, :] = u
        scale[rows, :] = jnp.broadcast_to(r, (CHUNK, TILE))
        low[rows, :] = (edges[rows, :].astype(f32) + u).astype(bf16)

    def block(start):
        return pl.ds(start, BLOCK)

    starts = range(0, e, BLOCK)
    late[0].wait()
    for at in starts:
        wide[block(at), :] = to_units(stacked[block(at), :], first)
        by_rows(at, activate)
    late[1].wait()
    for at in starts:
        wide[block(at), :] = from_units(low[block(at), :], second)
        by_rows(at, normalise)
    back = onehot_columns(receiver, n)
    aggregated = nn(back, low[...]).astype(bf16)

    preact_node = to_units(jnp.concatenate([nodes[...], aggregated], axis=1), node_first)
    s = sigmoid(preact_node)
    hidden_node = (preact_node * s).astype(bf16)
    node_unit, node_scale = normed(from_units(hidden_node, node_second))
    fresh[...] = (nodes[...].astype(f32) + node_unit).astype(bf16)
    out_copy = pltpu.make_async_copy(fresh, node_out, sems.at[2])
    out_copy.start()
    d_node_sum = normed_back(cotangent[...].astype(f32), node_unit, node_scale).astype(bf16)
    d_preact_node = (
        to_units(d_node_sum, node_second) * (s * (1.0 + preact_node * (1.0 - s)))
    ).astype(bf16)
    d_aggregated = from_units(d_preact_node, pl.ds(4 * d, d)).astype(bf16)
    own = units // 8
    lane = pl.multiple_of(lax.axis_index("y") * TILE, TILE)
    direct = cotangent[:, pl.ds(lane, TILE)].astype(f32) + from_units(
        d_preact_node, pl.ds(3 * d + lane, TILE)
    )
    direct = jnp.where(core == 0, direct[:, :own], direct[:, own : 2 * own])

    def denormalise(rows):
        low[rows, :] = normed_back(wide[rows, :], unit[rows, :], scale[rows, :1]).astype(bf16)

    def deactivate(rows):
        low[rows, :] = (wide[rows, :] * slope[rows, :]).astype(bf16)

    for at in starts:
        wide[block(at), :] = nn(received[block(at), :], d_aggregated)
        by_rows(at, denormalise)
    for at in starts:
        wide[block(at), :] = to_units(low[block(at), :], second)
        by_rows(at, deactivate)

    tails = jnp.concatenate(
        [weights[:, pl.ds(d + lane, TILE)], weights[:, pl.ds(2 * d + lane, TILE)]], axis=1
    )
    d_tails = nn(low[...], tails).astype(bf16)
    d_sender, d_receiver = d_tails[:, :TILE], d_tails[:, TILE:]
    table_grad = nn(onehot_columns(senders, n + h), d_sender)
    table_grad = jnp.where(core == 0, table_grad[:, :own], table_grad[:, own : 2 * own])
    receiver_grad = nn(back, d_receiver)
    base[...] = direct + table_grad[:n] + jnp.where(
        core == 0, receiver_grad[:, :own], receiver_grad[:, own : 2 * own]
    )
    d_own = jnp.where(core == 0, low[:, :own], low[:, own : 2 * own])
    grad = tn(d_own, stacked[...]).T.reshape(64, 3 * d // 64, own)
    both = jnp.concatenate([table_grad[n:].reshape(64, 8, own), grad], axis=1)
    outgoing[...] = jnp.concatenate([both[:, :16], both[:, 16:]], axis=2).astype(bf16)
    out_copy.wait()


def run_step(
    nodes, edges, cotangent, halo, pair, near, near_other, fars, sender, receivers
):
    n, d = nodes.shape
    e = edges.shape[0]
    h = halo.shape[0] // 2
    units = 4 * pair.shape[0]
    vmem = pl.BlockSpec(memory_space=pltpu.VMEM)
    anywhere = pl.BlockSpec(memory_space=pl.ANY)
    return pl.pallas_call(
        step_kernel,
        out_shape=(
            jax.ShapeDtypeStruct((n, d), bf16),
            jax.ShapeDtypeStruct((64, 16, TILE), bf16),
            jax.ShapeDtypeStruct((n, d // 8), f32),
        ),
        in_specs=[vmem] * 6 + [anywhere] + [vmem] * 3,
        out_specs=(anywhere, vmem, vmem),
        scratch_shapes=[
            pltpu.VMEM((n + h, d), bf16),
            pltpu.VMEM((e, 3 * d), bf16),
            pltpu.VMEM((e, units), f32),
            pltpu.VMEM((e, units), f32),
            pltpu.VMEM((e, d), f32),
            pltpu.VMEM((e, TILE), f32),
            pltpu.VMEM((e, units), bf16),
            pltpu.VMEM((e, n), bf16),
            pltpu.VMEM((units, pair.shape[1]), bf16),
            pltpu.VMEM((n, d), bf16),
            pltpu.SemaphoreType.DMA((3,)),
        ],
        compiler_params=pltpu.CompilerParams(vmem_limit_bytes=STEP_VMEM),
        name="step",
    )(nodes, edges, cotangent, halo, pair, near, near_other, fars, sender, receivers)


def finish_kernel(incoming, base, send, node_grad, first_grad):
    values = incoming[...].astype(f32)
    own = first_grad.shape[1]
    returned = values[:, :8, :own].reshape(values.shape[0] * 8, own).astype(bf16)
    hot = onehot_columns(flat_row(send[...]), base.shape[0])
    by_slot = tn(slot_order(*send.shape), returned).astype(bf16)
    part = (base[...] + nn(hot, by_slot)).astype(bf16)
    packed = jnp.concatenate([part[:TILE], part[TILE:]], axis=1)
    for share in range(node_grad.shape[0]):
        node_grad[share] = packed
    total = jnp.sum(values, axis=0)
    first_grad[...] = jnp.concatenate([total[8:, :own], total[:, own:]], axis=0)


def place_kernel(parts, node_grad):
    own = parts.shape[2] // 2
    for pair in range(parts.shape[0] // 2):
        low, high = parts[2 * pair], parts[2 * pair + 1]
        columns = pl.ds(pair * TILE, TILE)
        node_grad[:TILE, columns] = jnp.concatenate([low[:, :own], high[:, :own]], axis=1)
        node_grad[TILE:, columns] = jnp.concatenate([low[:, own:], high[:, own:]], axis=1)


def per_device(
    nodes,
    edges,
    node_cotangent,
    edge_first,
    edge_second,
    node_first,
    node_second,
    sender,
    receiver_pos,
    block_tile,
    live_blocks,
    send_rows,
):
    n, d = nodes.shape
    e = edges.shape[0]
    half = d // 2
    peers, slots = send_rows.shape[1], send_rows.shape[2]
    h = peers * slots
    columns = lax.axis_size("y")
    own = edge_second.shape[0]
    width = edge_first.shape[0] + node_first.shape[0] + 2 * d
    vmem = pl.BlockSpec(memory_space=pltpu.VMEM)
    send = send_rows[0].T

    supply, shard = pl.pallas_call(
        supply_kernel,
        out_shape=(
            jax.ShapeDtypeStruct((h, half), bf16),
            jax.ShapeDtypeStruct((own, width), bf16),
        ),
        in_specs=[vmem] * 6,
        out_specs=(vmem, vmem),
        compiler_params=pltpu.CompilerParams(vmem_limit_bytes=SUPPLY_VMEM),
        name="supply",
    )(nodes, send, edge_first.T, edge_second, node_first.T, node_second)
    pair = lax.all_gather(shard, "core", axis=0, tiled=True)
    beside = [
        (2 * i + c, 2 * ((i + (1, columns - 1)[c]) % columns) + c)
        for i in range(columns)
        for c in range(2)
    ]
    near = lax.ppermute(pair, ("y", "core"), beside)
    fars = lax.ppermute(near, ("y", "core"), beside)
    received = lax.all_to_all(
        supply.reshape(peers, slots, half), ("x", "z"), split_axis=0, concat_axis=0, tiled=True
    ).reshape(h, half)
    near_other = lax.ppermute(near, "core", [(0, 1), (1, 0)])
    halo = lax.all_gather(received, "core", axis=0, tiled=True)

    blocks = block_tile.shape[0]
    receivers = jnp.where(
        jnp.arange(blocks, dtype=jnp.int32)[:, None] < live_blocks,
        receiver_pos.reshape(blocks, TILE) + block_tile[:, None] * TILE,
        -1,
    )
    node_out, outgoing, base = run_step(
        nodes,
        edges,
        node_cotangent,
        halo,
        pair,
        near,
        near_other,
        fars,
        sender.reshape(blocks, TILE),
        receivers,
    )
    incoming = lax.all_to_all(outgoing, ("x", "z"), split_axis=0, concat_axis=0, tiled=True)
    copies, first_grad = pl.pallas_call(
        finish_kernel,
        out_shape=(
            jax.ShapeDtypeStruct((2 * columns, TILE, TILE), bf16),
            jax.ShapeDtypeStruct((edge_first.shape[0] // peers, own), f32),
        ),
        in_specs=[vmem] * 3,
        out_specs=(vmem, vmem),
        compiler_params=pltpu.CompilerParams(vmem_limit_bytes=FINISH_VMEM),
        name="finish",
    )(incoming, base, send)
    parts = lax.all_to_all(copies, ("y", "core"), split_axis=0, concat_axis=0, tiled=True)
    node_grad = pl.pallas_call(
        place_kernel,
        out_shape=jax.ShapeDtypeStruct((n, d), bf16),
        in_specs=[vmem],
        out_specs=vmem,
        compiler_params=pltpu.CompilerParams(vmem_limit_bytes=FINISH_VMEM),
        name="place",
    )(parts)
    return (node_out, node_grad, first_grad)


def solution(mesh):
    devices = mesh.devices
    tiles, shares = devices.shape
    fine = Mesh(devices.reshape(4, tiles // 4, shares // 2, 2), ("x", "z", "y", "core"))
    tile = ("x", "z")
    hid = ("y", "core")
    in_specs = (
        P(tile, None),
        P(tile, None),
        P(tile, None),
        P(None, hid),
        P(hid, None),
        P(None, hid),
        P(hid, None),
        P(tile),
        P(tile),
        P(tile),
        P(tile),
        P(tile, None, None),
    )
    out_specs = (P(tile, None), P(tile, None), P(tile, hid))
    return jax.shard_map(
        per_device, mesh=fine, in_specs=in_specs, out_specs=out_specs, check_vma=False
    )
```

```python
import jax
import jax.numpy as jnp
from jax import lax
from jax.experimental import pallas as pl
from jax.experimental.pallas import tpu as pltpu
from jax.sharding import Mesh, PartitionSpec as P

TILE = 128
epsilon = 1e-05
bf16 = jnp.bfloat16
f32 = jnp.float32
SUPPLY_VMEM = 60 * 1024 * 1024
STEP_VMEM = 24 * 1024 * 1024
FINISH_VMEM = 16 * 1024 * 1024
CHUNK = 16
BLOCK = 256


def nn(a, b):
    return lax.dot_general(a, b, (((1,), (0,)), ((), ())), preferred_element_type=f32)


def nt(a, b):
    return lax.dot_general(a, b, (((1,), (1,)), ((), ())), preferred_element_type=f32)


def tn(a, b):
    return lax.dot_general(a, b, (((0,), (0,)), ((), ())), preferred_element_type=f32)


def onehot_rows(index_row, count):
    n = index_row.shape[1]
    column = jnp.broadcast_to(index_row, (TILE, n)).T
    lanes = lax.broadcasted_iota(jnp.int32, (n, TILE), 1)
    return jnp.concatenate(
        [(column == lanes + k * TILE).astype(f32).astype(bf16) for k in range(count // TILE)],
        axis=1,
    )


def onehot_columns(index_row, count):
    n = index_row.shape[1]
    rows = lax.broadcasted_iota(jnp.int32, (count, n), 0)
    return (index_row == rows).astype(f32).astype(bf16)


def flat_row(rows):
    return jnp.concatenate([rows[i : i + 1] for i in range(rows.shape[0])], axis=1)


def slot_order(slots, peers):
    count = slots * peers
    bits = slots.bit_length() - 1
    row = lax.broadcasted_iota(jnp.int32, (count, TILE), 0)
    lanes = lax.broadcasted_iota(jnp.int32, (count, TILE), 1)
    source = (row & (slots - 1)) * peers + (row >> bits)
    return jnp.concatenate(
        [(source == lanes + k * TILE).astype(f32).astype(bf16) for k in range(count // TILE)],
        axis=1,
    )


def supply_kernel(nodes, send, first, second, node_first, node_second, supply, weights):
    core = lax.axis_index("core")
    half = nodes.shape[1] // 2
    hot = onehot_rows(flat_row(send[...]), nodes.shape[0])
    columns = pl.ds(pl.multiple_of(core * half, half), half)
    rows = nn(hot, nodes[:, columns]).astype(bf16)
    supply[...] = nn(slot_order(*send.shape), rows).astype(bf16)
    at = 0
    for part in (first, node_first, second, node_second):
        weights[:, at : at + part.shape[1]] = part[...]
        at += part.shape[1]


def sigmoid(v):
    return 0.5 * jnp.tanh(0.5 * v) + 0.5


def normed(v):
    centre = jnp.mean(v, axis=-1, keepdims=True)
    shifted = v - centre
    variance = jnp.mean(shifted * shifted, axis=-1, keepdims=True)
    scale = lax.rsqrt(variance + epsilon)
    return shifted * scale, scale


def normed_back(g, unit, scale):
    return scale * (
        g
        - jnp.mean(g, axis=-1, keepdims=True)
        - unit * jnp.mean(g * unit, axis=-1, keepdims=True)
    )


def by_rows(start, body):
    for at in range(start, start + BLOCK, CHUNK):
        body(pl.ds(at, CHUNK))


def step_kernel(
    nodes,
    edges,
    cotangent,
    halo,
    pair,
    near,
    near_other,
    fars,
    sender,
    receivers,
    node_out,
    outgoing,
    base,
    table,
    stacked,
    wide,
    slope,
    unit,
    scale,
    low,
    received,
    weights,
    fresh,
    sems,
):
    d = nodes.shape[1]
    half = d // 2
    n = nodes.shape[0]
    e = edges.shape[0]
    h = halo.shape[0] // 2
    core = lax.axis_index("core")
    first = pl.ds(0, 3 * d)
    node_first = pl.ds(3 * d, 2 * d)
    second = pl.ds(5 * d, d)
    node_second = pl.ds(6 * d, d)
    units = 4 * pair.shape[0]
    late = [
        pltpu.make_async_copy(
            near_other.at[:, columns],
            weights.at[pl.ds(units - pair.shape[0], pair.shape[0]), columns],
            sems.at[i],
        )
        for i, columns in enumerate((first, pl.ds(3 * d, 4 * d)))
    ]
    for copy in late:
        copy.start()
    for i, piece in enumerate((pair, near, fars)):
        weights[i * piece.shape[0] : (i + 1) * piece.shape[0], :] = piece[...]

    def to_units(x, columns):
        return nt(x, weights[:, columns])

    def from_units(x, columns):
        return nn(x, weights[:, columns])

    table[:n] = nodes[...]
    table[n:, :half] = halo[:h]
    table[n:, half:] = halo[h:]
    receiver = flat_row(receivers[...])
    received[...] = onehot_rows(receiver, n)
    senders = flat_row(sender[...])
    stacked[:, :d] = edges[...]
    stacked[:, d : 2 * d] = nn(onehot_rows(senders, n + h), table[...]).astype(bf16)
    stacked[:, 2 * d :] = nn(received[...], nodes[...]).astype(bf16)

    def activate(rows):
        v = wide[rows, :]
        s = sigmoid(v)
        low[rows, :] = (v * s).astype(bf16)
        slope[rows, :] = s * (1.0 + v * (1.0 - s))

    def normalise(rows):
        u, r = normed(wide[rows, :])
        unit[rows, :] = u
        scale[rows, :] = jnp.broadcast_to(r, (CHUNK, TILE))
        low[rows, :] = (edges[rows, :].astype(f32) + u).astype(bf16)

    def block(start):
        return pl.ds(start, BLOCK)

    starts = range(0, e, BLOCK)
    late[0].wait()
    for at in starts:
        wide[block(at), :] = to_units(stacked[block(at), :], first)
        by_rows(at, activate)
    late[1].wait()
    for at in starts:
        wide[block(at), :] = from_units(low[block(at), :], second)
        by_rows(at, normalise)
    back = onehot_columns(receiver, n)
    aggregated = nn(back, low[...]).astype(bf16)

    preact_node = to_units(jnp.concatenate([nodes[...], aggregated], axis=1), node_first)
    s = sigmoid(preact_node)
    hidden_node = (preact_node * s).astype(bf16)
    node_unit, node_scale = normed(from_units(hidden_node, node_second))
    fresh[...] = (nodes[...].astype(f32) + node_unit).astype(bf16)
    out_copy = pltpu.make_async_copy(fresh, node_out, sems.at[2])
    out_copy.start()
    d_node_sum = normed_back(cotangent[...].astype(f32), node_unit, node_scale).astype(bf16)
    d_preact_node = (
        to_units(d_node_sum, node_second) * (s * (1.0 + preact_node * (1.0 - s)))
    ).astype(bf16)
    d_aggregated = from_units(d_preact_node, pl.ds(4 * d, d)).astype(bf16)
    own = units // 8
    lane = pl.multiple_of(lax.axis_index("y") * TILE, TILE)
    direct = cotangent[:, pl.ds(lane, TILE)].astype(f32) + from_units(
        d_preact_node, pl.ds(3 * d + lane, TILE)
    )
    direct = jnp.where(core == 0, direct[:, :own], direct[:, own : 2 * own])

    def denormalise(rows):
        low[rows, :] = normed_back(wide[rows, :], unit[rows, :], scale[rows, :1]).astype(bf16)

    def deactivate(rows):
        low[rows, :] = (wide[rows, :] * slope[rows, :]).astype(bf16)

    for at in starts:
        wide[block(at), :] = nn(received[block(at), :], d_aggregated)
        by_rows(at, denormalise)
    for at in starts:
        wide[block(at), :] = to_units(low[block(at), :], second)
        by_rows(at, deactivate)

    tails = jnp.concatenate(
        [weights[:, pl.ds(d + lane, TILE)], weights[:, pl.ds(2 * d + lane, TILE)]], axis=1
    )
    d_tails = nn(low[...], tails).astype(bf16)
    d_sender, d_receiver = d_tails[:, :TILE], d_tails[:, TILE:]
    table_grad = nn(onehot_columns(senders, n + h), d_sender)
    table_grad = jnp.where(core == 0, table_grad[:, :own], table_grad[:, own : 2 * own])
    receiver_grad = nn(back, d_receiver)
    base[...] = direct + table_grad[:n] + jnp.where(
        core == 0, receiver_grad[:, :own], receiver_grad[:, own : 2 * own]
    )
    d_own = jnp.where(core == 0, low[:, :own], low[:, own : 2 * own])
    grad = tn(d_own, stacked[...]).T.reshape(64, 3 * d // 64, own)
    both = jnp.concatenate([table_grad[n:].reshape(64, 8, own), grad], axis=1)
    outgoing[...] = jnp.concatenate([both[:, :16], both[:, 16:]], axis=2).astype(bf16)
    out_copy.wait()


def run_step(
    nodes, edges, cotangent, halo, pair, near, near_other, fars, sender, receivers
):
    n, d = nodes.shape
    e = edges.shape[0]
    h = halo.shape[0] // 2
    units = 4 * pair.shape[0]
    vmem = pl.BlockSpec(memory_space=pltpu.VMEM)
    anywhere = pl.BlockSpec(memory_space=pl.ANY)
    return pl.pallas_call(
        step_kernel,
        out_shape=(
            jax.ShapeDtypeStruct((n, d), bf16),
            jax.ShapeDtypeStruct((64, 16, TILE), bf16),
            jax.ShapeDtypeStruct((n, d // 8), f32),
        ),
        in_specs=[vmem] * 6 + [anywhere] + [vmem] * 3,
        out_specs=(anywhere, vmem, vmem),
        scratch_shapes=[
            pltpu.VMEM((n + h, d), bf16),
            pltpu.VMEM((e, 3 * d), bf16),
            pltpu.VMEM((e, units), f32),
            pltpu.VMEM((e, units), f32),
            pltpu.VMEM((e, d), f32),
            pltpu.VMEM((e, TILE), f32),
            pltpu.VMEM((e, units), bf16),
            pltpu.VMEM((e, n), bf16),
            pltpu.VMEM((units, pair.shape[1]), bf16),
            pltpu.VMEM((n, d), bf16),
            pltpu.SemaphoreType.DMA((3,)),
        ],
        compiler_params=pltpu.CompilerParams(vmem_limit_bytes=STEP_VMEM),
        name="step",
    )(nodes, edges, cotangent, halo, pair, near, near_other, fars, sender, receivers)


def finish_kernel(incoming, base, send, node_grad, first_grad):
    values = incoming[...].astype(f32)
    own = first_grad.shape[1]
    returned = values[:, :8, :own].reshape(values.shape[0] * 8, own).astype(bf16)
    hot = onehot_columns(flat_row(send[...]), base.shape[0])
    by_slot = tn(slot_order(*send.shape), returned).astype(bf16)
    part = (base[...] + nn(hot, by_slot)).astype(bf16)
    packed = jnp.concatenate([part[:TILE], part[TILE:]], axis=1)
    for share in range(node_grad.shape[0]):
        node_grad[share] = packed
    total = jnp.sum(values, axis=0)
    first_grad[...] = jnp.concatenate([total[8:, :own], total[:, own:]], axis=0)


def place_kernel(parts, node_grad):
    own = parts.shape[2] // 2
    for pair in range(parts.shape[0] // 2):
        low, high = parts[2 * pair], parts[2 * pair + 1]
        columns = pl.ds(pair * TILE, TILE)
        node_grad[:TILE, columns] = jnp.concatenate([low[:, :own], high[:, :own]], axis=1)
        node_grad[TILE:, columns] = jnp.concatenate([low[:, own:], high[:, own:]], axis=1)


def per_device(
    nodes,
    edges,
    node_cotangent,
    edge_first,
    edge_second,
    node_first,
    node_second,
    sender,
    receiver_pos,
    block_tile,
    live_blocks,
    send_rows,
):
    n, d = nodes.shape
    e = edges.shape[0]
    half = d // 2
    peers, slots = send_rows.shape[1], send_rows.shape[2]
    h = peers * slots
    columns = lax.axis_size("y")
    own = edge_second.shape[0]
    width = edge_first.shape[0] + node_first.shape[0] + 2 * d
    vmem = pl.BlockSpec(memory_space=pltpu.VMEM)
    send = send_rows[0].T

    supply, shard = pl.pallas_call(
        supply_kernel,
        out_shape=(
            jax.ShapeDtypeStruct((h, half), bf16),
            jax.ShapeDtypeStruct((own, width), bf16),
        ),
        in_specs=[vmem] * 6,
        out_specs=(vmem, vmem),
        compiler_params=pltpu.CompilerParams(vmem_limit_bytes=SUPPLY_VMEM),
        name="supply",
    )(nodes, send, edge_first.T, edge_second, node_first.T, node_second)
    pair = lax.all_gather(shard, "core", axis=0, tiled=True)
    beside = [
        (2 * i + c, 2 * ((i + (1, columns - 1)[c]) % columns) + c)
        for i in range(columns)
        for c in range(2)
    ]
    near = lax.ppermute(pair, ("y", "core"), beside)
    fars = lax.ppermute(near, ("y", "core"), beside)
    received = lax.all_to_all(
        supply.reshape(peers, slots, half), ("x", "z"), split_axis=0, concat_axis=0, tiled=True
    ).reshape(h, half)
    near_other = lax.ppermute(near, "core", [(0, 1), (1, 0)])
    halo = lax.all_gather(received, "core", axis=0, tiled=True)

    blocks = block_tile.shape[0]
    receivers = jnp.where(
        jnp.arange(blocks, dtype=jnp.int32)[:, None] < live_blocks,
        receiver_pos.reshape(blocks, TILE) + block_tile[:, None] * TILE,
        -1,
    )
    node_out, outgoing, base = run_step(
        nodes,
        edges,
        node_cotangent,
        halo,
        pair,
        near,
        near_other,
        fars,
        sender.reshape(blocks, TILE),
        receivers,
    )
    incoming = lax.all_to_all(outgoing, ("x", "z"), split_axis=0, concat_axis=0, tiled=True)
    copies, first_grad = pl.pallas_call(
        finish_kernel,
        out_shape=(
            jax.ShapeDtypeStruct((2 * columns, TILE, TILE), bf16),
            jax.ShapeDtypeStruct((edge_first.shape[0] // peers, own), f32),
        ),
        in_specs=[vmem] * 3,
        out_specs=(vmem, vmem),
        compiler_params=pltpu.CompilerParams(vmem_limit_bytes=FINISH_VMEM),
        name="finish",
    )(incoming, base, send)
    parts = lax.all_to_all(copies, ("y", "core"), split_axis=0, concat_axis=0, tiled=True)
    node_grad = pl.pallas_call(
        place_kernel,
        out_shape=jax.ShapeDtypeStruct((n, d), bf16),
        in_specs=[vmem],
        out_specs=vmem,
        compiler_params=pltpu.CompilerParams(vmem_limit_bytes=FINISH_VMEM),
        name="place",
    )(parts)
    return (node_out, node_grad, first_grad)


def solution(mesh):
    devices = mesh.devices
    tiles, shares = devices.shape
    fine = Mesh(devices.reshape(4, tiles // 4, shares // 2, 2), ("x", "z", "y", "core"))
    tile = ("x", "z")
    hid = ("y", "core")
    in_specs = (
        P(tile, None),
        P(tile, None),
        P(tile, None),
        P(None, hid),
        P(hid, None),
        P(None, hid),
        P(hid, None),
        P(tile),
        P(tile),
        P(tile),
        P(tile),
        P(tile, None, None),
    )
    out_specs = (P(tile, None), P(tile, None), P(tile, hid))
    return jax.shard_map(
        per_device, mesh=fine, in_specs=in_specs, out_specs=out_specs, check_vma=False
    )
```
